256 devices in a mesh: stn: 64 (over y_hi, z, x), grp: 4 (over y_lo, core).
Axes of the slice: x: 4, y: 4 (y_hi: 2, y_lo: 2; y = y_hi * 2 + y_lo), z: 8, core: 2. Of those that a mesh axis runs over, the one named last changes fastest.
Arguments:
- voltages: bfloat16 [2, 128, 2, 180224], P(None, 'stn', None, 'grp'), may hold values from -6 to 6
- corr_taps: float32 [12, 4096], replicated, may hold values from -1.75 to 1.75
- beam_taps: float32 [12, 256], replicated, may hold values from -1.75 to 1.75
- angle_table: float32 [64, 256], replicated, may hold values from -3.140625 to 3.140625
- table_index: int32 [16, 128], replicated, may hold values from 0 to 63
Outputs:
- visibility: float32 [64, 256, 2, 256], P('stn', 'grp')
- beam_power: float32 [256, 16, 704], P('stn', None, 'grp')
The draws below stay inside these ranges and needn't reach their ends.
All inputs are finite; a program needn't handle non-finite values.
Results may differ from the reference program's by a relative error of at most 0.0046.
Values may be sent and summed in bfloat16 or wider, within the bound.
A program may use at most 128 MiB of HBM per device.

```python
import math
import jax
import jax.numpy as jnp
from jax import lax

S_DEV = 2
RADIX = 64
TAPS = 12
CH_B = 256
BEAMS = 16
TABLE = 64
STATIONS = 128
SIG = 256
CH = 4096
TIME = 180224
BIN_CH = 64
N_STN = 64


def plant(result, stream_key, smallest, high):
    shape = result.shape
    place = [jax.random.randint(jax.random.fold_in(stream_key, axis), (), 0, shape[axis]) for axis in range(len(shape))]
    result = result.at[tuple(place)].set(smallest)
    longest = shape.index(max(shape))
    place[longest] = (place[longest] + 1) % shape[longest]
    return result.at[tuple(place)].set(high)


def level_of(key, dims, pieces, smallest, high):
    loudness = 1.0
    for axis_at, shards_of in pieces:
        draws = jax.random.uniform(jax.random.fold_in(jax.random.fold_in(key, 6), axis_at), (shards_of,), jnp.float32, smallest / len(pieces), high / len(pieces))
        loudness = loudness * jnp.repeat(jnp.exp(draws), dims[axis_at] // shards_of).reshape((-1,) + (1,) * (len(dims) - 1 - axis_at))
    return loudness


def normal_values(own_key, extent, width, limit, cuts=(), kind=jnp.bfloat16):
    array = width * jax.random.normal(own_key, extent, jnp.float32)
    if cuts:
        array = array * level_of(own_key, extent, cuts, -0.22, 0.18)
    return jnp.clip(array, -limit, limit).astype(kind)


def setup_inputs(seed: int = 0) -> dict:
    key_of = jax.random.split(jax.random.key(seed), 6)
    voltages = normal_values(key_of[0], (2, STATIONS, 2, TIME), 1.0, 6.0, ((1, 64), (3, 4)))
    corr_taps = normal_values(key_of[1], (TAPS, CH), TAPS ** -0.5, 1.75, (), jnp.float32)
    beam_taps = normal_values(key_of[2], (TAPS, CH_B), TAPS ** -0.5, 1.75, (), jnp.float32)
    angle_table = jnp.clip(jax.random.uniform(key_of[3], (TABLE, CH_B), jnp.float32, -3.140625, 3.140625), -3.140625, 3.140625)
    table_index = plant(jax.random.randint(key_of[4], (BEAMS, STATIONS), 0, TABLE), jax.random.fold_in(key_of[4], 1), 0, TABLE - 1).astype(jnp.int32)
    return dict(voltages=voltages, corr_taps=corr_taps, beam_taps=beam_taps, angle_table=angle_table, table_index=table_index)


def dft_tables(length):
    positions = jnp.arange(length, dtype=jnp.int32)
    phases = (positions[:, None] * positions[None, :] % length).astype(jnp.float32) * (2.0 * math.pi / length)
    factor = 1.0 / math.sqrt(length)
    return ((jnp.cos(phases) * factor).astype(jnp.bfloat16), (jnp.sin(phases) * factor).astype(jnp.bfloat16))

def twiddles(radix_size):
    positions = jnp.arange(radix_size, dtype=jnp.int32)
    whole = radix_size * radix_size
    phases = (positions[:, None] * positions[None, :] % whole).astype(jnp.float32) * (2.0 * math.pi / whole)
    return (jnp.cos(phases), jnp.sin(phases))

def polyphase(extended, coefficients, frame_count):
    tap_count, length = coefficients.shape
    shaped = extended.reshape(extended.shape[:-1] + (frame_count + tap_count - 1, length))
    summed = jnp.zeros(shaped.shape[:-2] + (frame_count, length), jnp.float32)
    for tap_index in range(tap_count):
        lead_frame = tap_count - 1 - tap_index
        summed = summed + shaped[..., lead_frame:lead_frame + frame_count, :].astype(jnp.float32) * coefficients[tap_index]
    return summed.astype(jnp.bfloat16)

def contract(pattern, left_side, right_side):
    return jnp.einsum(pattern, left_side.astype(jnp.float32), right_side.astype(jnp.float32), precision=lax.Precision.HIGHEST)

def long_transform(real_part, imag_part):
    cos_table, sin_table = dft_tables(RADIX)
    twist_cos, twist_sin = twiddles(RADIX)
    split_shape = real_part.shape[:-1] + (RADIX, RADIX)
    real_part = real_part.reshape(split_shape)
    imag_part = imag_part.reshape(split_shape)
    first_form = '...ab,ak->...kb'
    middle_real = contract(first_form, real_part, cos_table) + contract(first_form, imag_part, sin_table)
    middle_imag = contract(first_form, imag_part, cos_table) - contract(first_form, real_part, sin_table)
    twisted_real = (middle_real * twist_cos + middle_imag * twist_sin).astype(jnp.bfloat16)
    twisted_imag = (middle_imag * twist_cos - middle_real * twist_sin).astype(jnp.bfloat16)
    second_form = '...kb,bm->...mk'
    result_real = contract(second_form, twisted_real, cos_table) + contract(second_form, twisted_imag, sin_table)
    result_imag = contract(second_form, twisted_imag, cos_table) - contract(second_form, twisted_real, sin_table)
    flat_shape = split_shape[:-2] + (RADIX * RADIX,)
    return (result_real.astype(jnp.bfloat16).reshape(flat_shape), result_imag.astype(jnp.bfloat16).reshape(flat_shape))

def short_transform(real_part, imag_part):
    cos_table, sin_table = dft_tables(real_part.shape[-1])
    pattern = '...n,nk->...k'
    result_real = contract(pattern, real_part, cos_table) + contract(pattern, imag_part, sin_table)
    result_imag = contract(pattern, imag_part, cos_table) - contract(pattern, real_part, sin_table)
    return (result_real.astype(jnp.bfloat16), result_imag.astype(jnp.bfloat16))

def beam_terms(weight_real, weight_imag, spec_real, spec_imag):
    pattern = 'bsc,sptc->cpbt'
    real_part = contract(pattern, weight_real, spec_real) - contract(pattern, weight_imag, spec_imag)
    imag_part = contract(pattern, weight_real, spec_imag) + contract(pattern, weight_imag, spec_real)
    return jnp.stack([real_part, imag_part], 1)

def reference(voltages, corr_taps, beam_taps, angle_table, table_index):
    tap_count = corr_taps.shape[0]
    angles = jnp.take(angle_table, table_index, axis=0)
    factor = 1.0 / math.sqrt(STATIONS)
    weight_real = (jnp.cos(angles) * factor).astype(jnp.bfloat16)
    weight_imag = (jnp.sin(angles) * factor).astype(jnp.bfloat16)
    frames = TIME // CH
    short_frames = TIME // CH_B

    def station_block(running, first_station):
        station_data = lax.dynamic_slice_in_dim(voltages, first_station, S_DEV, 1)
        padded = jnp.pad(station_data, ((0, 0), (0, 0), (0, 0), ((tap_count - 1) * CH, 0)))
        filtered = polyphase(padded, corr_taps, frames)
        spec_real, spec_imag = long_transform(filtered[0], filtered[1])
        short_input = padded[..., (tap_count - 1) * (CH - CH_B):]
        short_filtered = polyphase(short_input, beam_taps, short_frames)
        beam_real, beam_imag = short_transform(short_filtered[0], short_filtered[1])
        part_real = lax.dynamic_slice_in_dim(weight_real, first_station, S_DEV, 1)
        part_imag = lax.dynamic_slice_in_dim(weight_imag, first_station, S_DEV, 1)
        running = running + beam_terms(part_real, part_imag, beam_real, beam_imag)
        return (running, (spec_real, spec_imag))
    starts = jnp.arange(N_STN, dtype=jnp.int32) * S_DEV
    initial = jnp.zeros((CH_B, 2, 2, BEAMS, short_frames), jnp.float32)
    beam_fields, (spec_real, spec_imag) = lax.scan(station_block, initial, starts)
    spec_real = spec_real.reshape(SIG, frames, CH)
    spec_imag = spec_imag.reshape(SIG, frames, CH)

    def one_bin(first_channel):
        part_real = lax.dynamic_slice_in_dim(spec_real, first_channel, BIN_CH, 2).reshape(SIG, frames * BIN_CH)
        part_imag = lax.dynamic_slice_in_dim(spec_imag, first_channel, BIN_CH, 2).reshape(SIG, frames * BIN_CH)
        stacked = jnp.concatenate([part_real, part_imag], 1)
        rotated = jnp.concatenate([part_imag, -part_real], 1)
        real_part = jnp.dot(stacked, stacked.T, preferred_element_type=jnp.float32)
        imag_part = jnp.dot(rotated, stacked.T, preferred_element_type=jnp.float32)
        return jnp.stack([real_part, imag_part], 1)
    summed = lax.map(one_bin, jnp.arange(N_STN, dtype=jnp.int32) * BIN_CH)
    visibility = summed * (1.0 / math.sqrt(frames * BIN_CH))
    beam_power = lax.optimization_barrier(jnp.sum(beam_fields[:, 0] ** 2 + beam_fields[:, 1] ** 2, axis=1))
    return (visibility, beam_power)
```

```python
import math

import jax
import jax.numpy as jnp
from jax import lax
from jax.sharding import PartitionSpec as P

RADIX = 64


def from_behind(array, axis, by):
    devices = lax.axis_size(axis)
    pairs = [(i, i + by) for i in range(devices) if 0 <= i + by < devices]
    return lax.ppermute(array, axis, pairs)


def dft_tables(length):
    positions = jnp.arange(length, dtype=jnp.int32)
    phases = (positions[:, None] * positions[None, :] % length).astype(jnp.float32) * (
        2.0 * math.pi / length
    )
    factor = 1.0 / math.sqrt(length)
    return (
        (jnp.cos(phases) * factor).astype(jnp.bfloat16),
        (jnp.sin(phases) * factor).astype(jnp.bfloat16),
    )


def twiddles(radix_size):
    positions = jnp.arange(radix_size, dtype=jnp.int32)
    whole = radix_size * radix_size
    phases = (positions[:, None] * positions[None, :] % whole).astype(jnp.float32) * (
        2.0 * math.pi / whole
    )
    return (jnp.cos(phases), jnp.sin(phases))


def polyphase(extended, coefficients, frame_count):
    tap_count, length = coefficients.shape
    shaped = extended.reshape(extended.shape[:-1] + (frame_count + tap_count - 1, length))
    summed = jnp.zeros(shaped.shape[:-2] + (frame_count, length), jnp.float32)
    for tap_index in range(tap_count):
        lead_frame = tap_count - 1 - tap_index
        summed = (
            summed
            + shaped[..., lead_frame : lead_frame + frame_count, :].astype(jnp.float32)
            * coefficients[tap_index]
        )
    return summed.astype(jnp.bfloat16)


def contract(pattern, left_side, right_side):
    return jnp.einsum(pattern, left_side, right_side, preferred_element_type=jnp.float32)


def long_transform(real_part, imag_part):
    cos_table, sin_table = dft_tables(RADIX)
    twist_cos, twist_sin = twiddles(RADIX)
    split_shape = real_part.shape[:-1] + (RADIX, RADIX)
    real_part = real_part.reshape(split_shape)
    imag_part = imag_part.reshape(split_shape)
    first_form = "...ab,ak->...kb"
    middle_real = contract(first_form, real_part, cos_table) + contract(
        first_form, imag_part, sin_table
    )
    middle_imag = contract(first_form, imag_part, cos_table) - contract(
        first_form, real_part, sin_table
    )
    twisted_real = (middle_real * twist_cos + middle_imag * twist_sin).astype(jnp.bfloat16)
    twisted_imag = (middle_imag * twist_cos - middle_real * twist_sin).astype(jnp.bfloat16)
    second_form = "...kb,bm->...mk"
    result_real = contract(second_form, twisted_real, cos_table) + contract(
        second_form, twisted_imag, sin_table
    )
    result_imag = contract(second_form, twisted_imag, cos_table) - contract(
        second_form, twisted_real, sin_table
    )
    flat_shape = split_shape[:-2] + (RADIX * RADIX,)
    return jnp.stack(
        [
            result_real.astype(jnp.bfloat16).reshape(flat_shape),
            result_imag.astype(jnp.bfloat16).reshape(flat_shape),
        ],
        0,
    )


def short_transform(real_part, imag_part):
    cos_table, sin_table = dft_tables(real_part.shape[-1])
    pattern = "...n,nk->...k"
    result_real = contract(pattern, real_part, cos_table) + contract(pattern, imag_part, sin_table)
    result_imag = contract(pattern, imag_part, cos_table) - contract(pattern, real_part, sin_table)
    return jnp.stack([result_real.astype(jnp.bfloat16), result_imag.astype(jnp.bfloat16)], 0)


def station_weights(index_rows, columns, station_total):
    table_rows = jnp.arange(columns.shape[0], dtype=jnp.int32)
    one_hot = (index_rows[..., None] == table_rows).astype(jnp.float32)
    angles = jnp.einsum("bst,tc->bsc", one_hot, columns, precision=lax.Precision.HIGHEST)
    factor = 1.0 / math.sqrt(station_total)
    return (
        (jnp.cos(angles) * factor).astype(jnp.bfloat16),
        (jnp.sin(angles) * factor).astype(jnp.bfloat16),
    )


def on_device(voltages, corr_taps, beam_taps, angle_table, table_index):
    tap_count = corr_taps.shape[0]
    length = corr_taps.shape[1]
    short_length = beam_taps.shape[1]
    local_stations = voltages.shape[1]
    samples = voltages.shape[3]
    station_total = local_stations * lax.axis_size("stn")
    history = from_behind(voltages, "grp", 1)
    extended = jnp.concatenate([history, voltages], 3)
    filtered = polyphase(extended, corr_taps, samples // length)
    spectra = long_transform(filtered[0], filtered[1])
    short_input = extended[..., (tap_count - 1) * (length - short_length) :]
    short_filtered = polyphase(short_input, beam_taps, samples // short_length)
    short_spectra = short_transform(short_filtered[0], short_filtered[1])
    turned = lax.all_to_all(spectra, "stn", split_axis=4, concat_axis=1, tiled=True)
    moved = lax.all_to_all(
        short_spectra.transpose(4, 0, 1, 2, 3), "stn", split_axis=0, concat_axis=2, tiled=True
    )
    own_channels = short_length // lax.axis_size("stn")
    own_columns = lax.dynamic_slice_in_dim(
        angle_table, lax.axis_index("stn") * own_channels, own_channels, 1
    )
    weight_real, weight_imag = station_weights(table_index, own_columns, station_total)
    spec_real, spec_imag = moved[:, 0], moved[:, 1]
    pattern = "bsc,cspt->cpbt"
    beam_real = contract(pattern, weight_real, spec_real) - contract(
        pattern, weight_imag, spec_imag
    )
    beam_imag = contract(pattern, weight_real, spec_imag) + contract(
        pattern, weight_imag, spec_real
    )
    beam_power = jnp.sum(beam_real**2 + beam_imag**2, axis=1)
    signals = turned.shape[1] * turned.shape[2]
    inner_depth = turned.shape[3] * turned.shape[4]
    flat_real = turned[0].reshape(signals, inner_depth)
    flat_imag = turned[1].reshape(signals, inner_depth)
    stacked = jnp.concatenate([flat_real, flat_imag], 1)
    rotated = jnp.concatenate([flat_imag, -flat_real], 1)
    real_part = lax.dot_general(
        stacked, stacked, (((1,), (1,)), ((), ())), preferred_element_type=jnp.float32
    )
    imag_part = lax.dot_general(
        rotated, stacked, (((1,), (1,)), ((), ())), preferred_element_type=jnp.float32
    )
    summed = lax.psum_scatter(
        jnp.stack([real_part, imag_part], 1), "grp", scatter_dimension=0, tiled=True
    )
    visibility = (summed * (1.0 / math.sqrt(inner_depth * lax.axis_size("grp"))))[None]
    return (visibility, beam_power)


def solution(mesh):
    in_specs = (P(None, "stn", None, "grp"), P(), P(), P(), P())
    out_specs = (P("stn", "grp", None, None), P("stn", None, "grp"))
    return jax.shard_map(
        on_device, mesh=mesh, in_specs=in_specs, out_specs=out_specs, check_vma=False
    )
```

```python
import functools
import math

import jax
import jax.numpy as jnp
import ml_dtypes
import numpy as np
from jax import lax
from jax.experimental import pallas as pl
from jax.experimental.pallas import tpu as pltpu
from jax.sharding import PartitionSpec as P

MESH = pl.DeviceIdType.MESH
BF = jnp.bfloat16
F32 = jnp.float32

RADIX = 64
TAPS = 12
STN = 64
GRP = 4
LANES = 128
TILES = 352
HALF = 176
FRAMES = 11
SHORT_FRAMES = 176
SHORT_HALO = 22
BEAM_LANES = 384


def dft_tables(length):
    k = np.arange(length)
    phases = (k[:, None] * k[None, :] % length) * (2.0 * math.pi / length)
    factor = 1.0 / math.sqrt(length)
    return np.cos(phases) * factor, np.sin(phases) * factor


def constant_tables():
    bf = ml_dtypes.bfloat16
    cos, sin = dft_tables(RADIX)
    order = np.concatenate([np.arange(0, RADIX, 2), np.arange(1, RADIX, 2)])
    c, s = cos[order].T, sin[order].T
    first = np.block([[c, s], [-s, c]])
    k = np.arange(RADIX)
    phases = (k[:, None] * k[None, :]) * (2.0 * math.pi / (RADIX * RADIX))
    twist = np.stack([np.tile(np.cos(phases), (1, 4)), np.tile(np.sin(phases), (1, 4))])
    second = np.zeros((RADIX, 4, 2, 2, 4, RADIX))
    for q in range(4):
        second[:, q, 0, 0, q] = cos.T
        second[:, q, 0, 1, q] = sin.T
        second[:, q, 1, 0, q] = -sin.T
        second[:, q, 1, 1, q] = cos.T
    second = second.reshape(512, 512)
    cos, sin = dft_tables(256)
    short = np.zeros((256, 2, 2, 256))
    short[:, 0, 0] = cos.T
    short[:, 0, 1] = sin.T
    short[:, 1, 0] = -sin.T
    short[:, 1, 1] = cos.T
    short = short.reshape(512, 512)
    pick = np.zeros((2, 384, 16, 2, 4, 2))
    for pair in range(2):
        for src in range(16):
            for q in range(4):
                u = src * 4 + q
                pick[pair, 2 * u, src, pair, q, 0] = 1
                pick[pair, 2 * u + 1, src, pair, q, 1] = 1
                pick[pair, 128 + 2 * u, src, pair, q, 1] = 1
                pick[pair, 128 + 2 * u + 1, src, pair, q, 0] = -1
                pick[pair, 256 + u, src, pair, q, 0] = 1
                pick[pair, 320 + u, src, pair, q, 1] = 1
    pick = pick.reshape(768, 256)
    return (
        first.astype(bf),
        twist.astype(np.float32),
        second.astype(bf),
        short.astype(bf),
        pick.astype(bf),
    )


def dot(a, b):
    return lax.dot_general(a, b, (((1,), (0,)), ((), ())), preferred_element_type=F32)


def dot_t(a, b):
    return lax.dot_general(a, b, (((1,), (1,)), ((), ())), preferred_element_type=F32)


def partner(stn, offset):
    y = lax.rem(stn // 32 + offset // 32, 2)
    z = lax.rem(lax.rem(stn // 4, 8) + lax.rem(offset // 4, 8), 8)
    x = lax.rem(lax.rem(stn, 4) + lax.rem(offset, 4), 4)
    return y * 32 + z * 4 + x


def kernel(
    x_ref, corr_taps, beam_taps, angles, index, first, twist, second, short, pick,
    vis_ref, power_ref,
    hist, ext, fs, fl, z_ref, tw, send_beam, recv_beam, send_spec, recv_spec,
    table, weights, lhs, rhs, part_own, part_send, part_recv,
    halo_send, halo_recv, beam_send_sem, beam_recv_sem, spec_send_sem, spec_recv_sem,
    part_send_sem, part_recv_sem, local_sem,
):
    stn = lax.axis_index("stn")
    grp = lax.axis_index("grp")

    barrier = pltpu.get_barrier_semaphore()

    def greet(k, _):
        pl.semaphore_signal(
            barrier, inc=1, device_id=(partner(stn, k), grp), device_id_type=MESH
        )
        return 0

    lax.fori_loop(1, STN, greet, 0)
    for k in range(1, GRP):
        pl.semaphore_signal(
            barrier, inc=1, device_id=(stn, lax.rem(grp + k, GRP)), device_id_type=MESH
        )

    def widen(source, at, first_tile):
        def body(i, _):
            v = source[i].astype(F32)
            ext[at + i] = v[:8]
            ext[at + HALF + i] = v[8:]
            return 0

        lax.fori_loop(first_tile, HALF, body, 0, unroll=8)

    widen(x_ref, TILES, 0)
    pl.semaphore_wait(barrier, STN - 1 + GRP - 1)

    def halo(i):
        at = pl.ds(HALF - SHORT_HALO, SHORT_HALO) if i == 0 else pl.ds(0, HALF - SHORT_HALO)
        return pltpu.make_async_remote_copy(
            src_ref=x_ref.at[at],
            dst_ref=hist.at[at],
            send_sem=halo_send.at[i],
            recv_sem=halo_recv.at[i],
            device_id=(stn, lax.rem(grp + 1, GRP)),
            device_id_type=MESH,
        )

    @pl.when(grp < GRP - 1)
    def _():
        halo(0).start()
        halo(1).start()

    @pl.when(grp == 0)
    def _():
        def clear(i, _):
            ext[i] = jnp.zeros((8, LANES), F32)
            return 0

        lax.fori_loop(0, TILES, clear, 0, unroll=8)

    @pl.when(grp > 0)
    def _():
        halo(0).wait_recv()
        widen(hist, 0, HALF - SHORT_HALO)

    step = 8

    def short_filter(i, _):
        for a in range(2):
            taps = [
                jnp.broadcast_to(beam_taps[pl.ds(k, 1), a * LANES : (a + 1) * LANES], (8, LANES))
                for k in range(TAPS)
            ]
            base = TILES + i * (2 * step) + a
            window = [ext[base + 2 * j] for j in range(1 - TAPS, step)]
            for f in range(step):
                total = window[f + TAPS - 1] * taps[0]
                for k in range(1, TAPS):
                    total = total + window[f + TAPS - 1 - k] * taps[k]
                fs[a, pl.ds(pl.multiple_of((i * step + f) * 8, 8), 8), :] = total
        return 0

    lax.fori_loop(0, SHORT_FRAMES // step, short_filter, 0)
    halves = []
    for st in range(2):
        for p in range(2):
            for part in range(2):
                for a in range(2):
                    z_ref[pl.ds(p * SHORT_FRAMES, SHORT_FRAMES), pl.ds(part * 256 + a * LANES, LANES)] = fs[
                        a, pl.ds(part * 4 + st * 2 + p, SHORT_FRAMES, stride=8), :
                    ].astype(BF)
        z_ref[pl.ds(2 * SHORT_FRAMES, BEAM_LANES - 2 * SHORT_FRAMES), :] = jnp.zeros(
            (BEAM_LANES - 2 * SHORT_FRAMES, 512), BF
        )
        halves.append(dot_t(short[...], z_ref[...]).reshape(STN, 8, BEAM_LANES))
    send_beam[...] = jnp.concatenate(halves, axis=1).astype(BF)

    def exchange(source, target, send_sem, recv_sem, k):
        other = partner(stn, k)
        return pltpu.make_async_remote_copy(
            src_ref=source.at[other],
            dst_ref=target.at[stn],
            send_sem=send_sem,
            recv_sem=recv_sem,
            device_id=(other, grp),
            device_id_type=MESH,
        )

    def send_all(source, target, send_sem, recv_sem):
        def body(k, _):
            exchange(source, target, send_sem, recv_sem, k).start()
            return 0

        lax.fori_loop(1, STN, body, 0)

    def wait_all(source, target, send_sem, recv_sem):
        span = pl.ds(0, STN - 1)
        pltpu.make_async_copy(source.at[span], target.at[span], recv_sem).wait()

    def wait_sent(source, target, send_sem, recv_sem):
        span = pl.ds(0, STN - 1)
        pltpu.make_async_copy(source.at[span], target.at[span], send_sem).wait()

    beam_args = (send_beam, recv_beam, beam_send_sem, beam_recv_sem)
    spec_args = (send_spec, recv_spec, spec_send_sem, spec_recv_sem)
    send_all(*beam_args)
    recv_beam[stn] = send_beam[stn]

    @pl.when(grp > 0)
    def _():
        halo(1).wait_recv()

        def body(i, _):
            v = hist[i].astype(F32)
            ext[i] = v[:8]
            ext[HALF + i] = v[8:]
            return 0

        lax.fori_loop(0, HALF - SHORT_HALO, body, 0, unroll=7)

    def long_filter(i, _):
        taps = [
            jnp.broadcast_to(
                corr_taps[pl.ds(k, 1), pl.ds(pl.multiple_of(i * LANES, LANES), LANES)], (8, LANES)
            )
            for k in range(TAPS)
        ]
        window = [ext[i + 32 * j] for j in range(2 * FRAMES)]
        for g in range(FRAMES):
            total = window[g + TAPS - 1] * taps[0]
            for k in range(1, TAPS):
                total = total + window[g + TAPS - 1 - k] * taps[k]
            fl[pl.ds(pl.multiple_of((g * 32 + i) * 8, 8), 8), :] = total
        return 0

    lax.fori_loop(0, 32, long_filter, 0)

    low = lax.broadcasted_iota(jnp.int32, (32, LANES), 1) < RADIX

    def first_factor(g, _):
        rows = []
        for part in range(2):
            even, odd = [], []
            for q2 in range(2):
                a = fl[pl.ds(g * 256 + part * 4 + 2 * q2, 32, stride=8), :]
                b = fl[pl.ds(g * 256 + part * 4 + 2 * q2 + 1, 32, stride=8), :]
                even.append(jnp.where(low, a, pltpu.roll(b, RADIX, 1)))
                odd.append(jnp.where(low, pltpu.roll(a, RADIX, 1), b))
            rows.append(jnp.concatenate(even, axis=1))
            rows.append(jnp.concatenate(odd, axis=1))
        out = dot(first[...], jnp.concatenate(rows, axis=0).astype(BF))
        real, imag = out[:RADIX], out[RADIX:]
        at = pl.ds(pl.multiple_of(g * RADIX, RADIX), RADIX)
        tw[at, 0:256] = (real * twist[0] + imag * twist[1]).astype(BF)
        tw[at, 256:512] = (imag * twist[0] - real * twist[1]).astype(BF)
        return 0

    lax.fori_loop(0, FRAMES, first_factor, 0)
    tw[FRAMES * RADIX : 12 * RADIX, :] = jnp.zeros((RADIX, 512), BF)

    for gpp in range(3):
        pairs = [
            dot_t(second[...], tw[(2 * gpp + e) * LANES : (2 * gpp + e + 1) * LANES, :]).reshape(STN, 8, LANES)
            for e in range(2)
        ]
        send_spec[:, 16 * gpp : 16 * gpp + 16, :] = jnp.concatenate(pairs, axis=1).astype(BF)

    send_all(*spec_args)
    recv_spec[stn] = send_spec[stn]

    shape = (256, 1024)
    column = lax.broadcasted_iota(jnp.int32, shape, 1)
    match = lax.broadcasted_iota(jnp.int32, shape, 0) == stn * 4 + (column // 2) % 4
    own_re = jnp.where(match & (column % 2 == 0), 1.0, 0.0).astype(BF)
    own_im = jnp.where(match & (column % 2 == 1), 1.0, 0.0).astype(BF)
    factor = 1.0 / math.sqrt(2 * STN)
    cos = (jnp.cos(angles[...]) * factor).astype(BF)
    sin = (jnp.sin(angles[...]) * factor).astype(BF)
    table[0] = dot(cos, own_re) - dot(sin, own_im)
    table[1] = dot(sin, own_re) + dot(cos, own_im)
    shape = (128, 1024)
    spread = jnp.where(
        lax.broadcasted_iota(jnp.int32, shape, 0) == lax.broadcasted_iota(jnp.int32, shape, 1) // 8,
        1.0,
        0.0,
    ).astype(BF)
    chosen = dot(index[...].astype(F32).astype(BF), spread)

    def choose(t, carry):
        real, imag = carry
        hit = chosen == t.astype(F32)
        return (
            jnp.where(hit, jnp.broadcast_to(table[0, pl.ds(t, 1), :], (16, 1024)), real),
            jnp.where(hit, jnp.broadcast_to(table[1, pl.ds(t, 1), :], (16, 1024)), imag),
        )

    zero = jnp.zeros((16, 1024), F32)
    chosen_parts = lax.fori_loop(0, 64, choose, (zero, zero))
    channel = (lax.broadcasted_iota(jnp.int32, (16, 1024), 1) // 2) % 4
    for po in range(2):
        for ci in range(4):
            weights[po * 64 + ci * 16 : po * 64 + ci * 16 + 16, :] = jnp.where(
                channel == ci, chosen_parts[po], 0.0
            ).astype(BF)

    wait_all(*beam_args)
    fields = dot(weights[...], recv_beam[...].reshape(1024, BEAM_LANES))
    power = fields[:64] * fields[:64] + fields[64:] * fields[64:]
    power_ref[...] = power[:, 0:SHORT_FRAMES] + power[:, SHORT_FRAMES : 2 * SHORT_FRAMES]

    wait_all(*spec_args)

    def gather_rows(b, _):
        for gpp in range(3):
            block = recv_spec[pl.ds(b * 16, 16), 16 * gpp : 16 * gpp + 16, :].reshape(256, LANES)
            rows = dot(pick[...], block).astype(BF)
            for e in range(2):
                at = 384 * e
                lanes = (2 * gpp + e) * LANES
                wide = pl.ds(pl.multiple_of(b * 128, 128), 128)
                narrow = pl.ds(pl.multiple_of(b * 64, 64), 64)
                lhs[wide, lanes : lanes + LANES] = rows[at : at + 128]
                lhs[wide, 768 + lanes : 768 + lanes + LANES] = rows[at + 128 : at + 256]
                rhs[narrow, lanes : lanes + LANES] = rows[at + 256 : at + 320]
                rhs[narrow, 768 + lanes : 768 + lanes + LANES] = rows[at + 320 : at + 384]
        return 0

    lax.fori_loop(0, 4, gather_rows, 0)
    for i in range(GRP):
        partial = dot_t(lhs[i * 128 : i * 128 + 128, :], rhs[...])
        part_own[i] = partial
        part_send[i] = partial.astype(BF)

    def hand_over(k):
        other = lax.rem(grp + k, GRP)
        return pltpu.make_async_remote_copy(
            src_ref=part_send.at[other],
            dst_ref=part_recv.at[k - 1],
            send_sem=part_send_sem.at[k - 1],
            recv_sem=part_recv_sem.at[k - 1],
            device_id=(stn, other),
            device_id_type=MESH,
        )

    for k in range(1, GRP):
        hand_over(k).start()
    total = part_own[grp]
    for k in range(1, GRP):
        hand_over(k).wait_recv()
        total = total + part_recv[k - 1].astype(F32)
    vis_ref[...] = total * (1.0 / math.sqrt(4 * FRAMES * RADIX))

    for k in range(1, GRP):
        hand_over(k).wait_send()
    wait_sent(*beam_args)
    wait_sent(*spec_args)

    @pl.when(grp < GRP - 1)
    def _():
        halo(0).wait_send()
        halo(1).wait_send()


def on_device(voltages, corr_taps, beam_taps, angle_table, table_index):
    x = voltages.reshape(8, 2, HALF, LANES).transpose(2, 1, 0, 3).reshape(HALF, 16, LANES)
    tables = [jnp.asarray(t) for t in constant_tables()]
    vmem = pl.BlockSpec(memory_space=pltpu.VMEM)
    dma = pltpu.SemaphoreType.DMA
    vis, power = pl.pallas_call(
        kernel,
        out_shape=(
            jax.ShapeDtypeStruct((128, 256), F32),
            jax.ShapeDtypeStruct((64, SHORT_FRAMES), F32),
        ),
        in_specs=[vmem] * 10,
        out_specs=(vmem, vmem),
        scratch_shapes=[
            pltpu.VMEM((HALF, 16, LANES), BF),
            pltpu.VMEM((2 * TILES, 8, LANES), F32),
            pltpu.VMEM((2, SHORT_FRAMES * 8, LANES), F32),
            pltpu.VMEM((FRAMES * 256, LANES), F32),
            pltpu.VMEM((BEAM_LANES, 512), BF),
            pltpu.VMEM((12 * RADIX, 512), BF),
            pltpu.VMEM((STN, 16, BEAM_LANES), BF),
            pltpu.VMEM((STN, 16, BEAM_LANES), BF),
            pltpu.VMEM((STN, 48, LANES), BF),
            pltpu.VMEM((STN, 48, LANES), BF),
            pltpu.VMEM((2, 64, 1024), F32),
            pltpu.VMEM((128, 1024), BF),
            pltpu.VMEM((512, 1536), BF),
            pltpu.VMEM((256, 1536), BF),
            pltpu.VMEM((GRP, 128, 256), F32),
            pltpu.VMEM((GRP, 128, 256), BF),
            pltpu.VMEM((GRP - 1, 128, 256), BF),
            dma((2,)),
            dma((2,)),
            dma,
            dma,
            dma,
            dma,
            dma((GRP - 1,)),
            dma((GRP - 1,)),
            dma,
        ],
        compiler_params=pltpu.CompilerParams(
            collective_id=0, has_side_effects=True, vmem_limit_bytes=48 * 1024 * 1024
        ),
    )(x, corr_taps, beam_taps, angle_table, table_index, *tables)
    return vis.reshape(1, 64, 2, 256), power.reshape(4, 16, SHORT_FRAMES)


def solution(mesh):
    in_specs = (P(None, "stn", None, "grp"), P(), P(), P(), P())
    out_specs = (P("stn", "grp", None, None), P("stn", None, "grp"))
    return jax.shard_map(
        on_device, mesh=mesh, in_specs=in_specs, out_specs=out_specs, check_vma=False
    )
```

```python
import functools
import math

import jax
import jax.numpy as jnp
import ml_dtypes
import numpy as np
from jax import lax
from jax.experimental import pallas as pl
from jax.experimental.pallas import tpu as pltpu
from jax.sharding import PartitionSpec as P

MESH = pl.DeviceIdType.MESH
BF = jnp.bfloat16
F32 = jnp.float32

RADIX = 64
TAPS = 12
STN = 64
GRP = 4
LANES = 128
TILES = 352
HALF = 176
FRAMES = 11
SHORT_FRAMES = 176
FRAMES_B = 48
FRAMES_A = SHORT_FRAMES - FRAMES_B


def dft_tables(length):
    k = np.arange(length)
    phases = (k[:, None] * k[None, :] % length) * (2.0 * math.pi / length)
    factor = 1.0 / math.sqrt(length)
    return np.cos(phases) * factor, np.sin(phases) * factor


def constant_tables():
    bf = ml_dtypes.bfloat16
    cos, sin = dft_tables(RADIX)
    order = np.concatenate([np.arange(0, RADIX, 2), np.arange(1, RADIX, 2)])
    c, s = cos[order].T, sin[order].T
    first = np.block([[c, s], [-s, c]])
    k = np.arange(RADIX)
    phases = (k[:, None] * k[None, :]) * (2.0 * math.pi / (RADIX * RADIX))
    twist = np.stack([np.tile(np.cos(phases), (1, 4)), np.tile(np.sin(phases), (1, 4))])
    second = np.zeros((RADIX, 4, 2, 2, 4, RADIX))
    for q in range(4):
        second[:, q, 0, 0, q] = cos.T
        second[:, q, 0, 1, q] = sin.T
        second[:, q, 1, 0, q] = -sin.T
        second[:, q, 1, 1, q] = cos.T
    second = second.reshape(512, 512)
    cos, sin = dft_tables(256)
    short = np.zeros((256, 2, 2, 256))
    short[:, 0, 0] = cos.T
    short[:, 0, 1] = sin.T
    short[:, 1, 0] = -sin.T
    short[:, 1, 1] = cos.T
    short = short.reshape(512, 512)
    pick = np.zeros((2, 384, 16, 2, 4, 2))
    for pair in range(2):
        for src in range(16):
            for q in range(4):
                u = src * 4 + q
                pick[pair, 2 * u, src, pair, q, 0] = 1
                pick[pair, 2 * u + 1, src, pair, q, 1] = 1
                pick[pair, 128 + 2 * u, src, pair, q, 1] = 1
                pick[pair, 128 + 2 * u + 1, src, pair, q, 0] = -1
                pick[pair, 256 + u, src, pair, q, 0] = 1
                pick[pair, 320 + u, src, pair, q, 1] = 1
    pick = pick.reshape(768, 256)
    return (
        first.astype(bf),
        twist.astype(np.float32),
        second.astype(bf),
        short.astype(bf),
        pick.astype(bf),
    )


def dot(a, b):
    return lax.dot_general(a, b, (((1,), (0,)), ((), ())), preferred_element_type=F32)


def dot_t(a, b):
    return lax.dot_general(a, b, (((1,), (1,)), ((), ())), preferred_element_type=F32)


def partner(stn, offset):
    y = lax.rem(stn // 32 + offset // 32, 2)
    z = lax.rem(lax.rem(stn // 4, 8) + lax.rem(offset // 4, 8), 8)
    x = lax.rem(lax.rem(stn, 4) + lax.rem(offset, 4), 4)
    return y * 32 + z * 4 + x


def kernel(
    x_ref, corr_taps, beam_taps, angles, index, first, twist, second_hbm, short_hbm, pick_hbm,
    vis_ref, power_ref,
    second, short, pick,
    hist, ext, fs, fl, z_ref, tw, send_a, recv_a, send_b, recv_b, send_spec, recv_spec,
    table, weights, lhs, rhs, part_own, part_send, part_recv,
    row_sem, column_sem, table_sem, halo_send, halo_recv,
    a_send_sem, a_recv_sem, b_send_sem, b_recv_sem, spec_send_sem, spec_recv_sem,
    part_send_sem, part_recv_sem,
):
    stn = lax.axis_index("stn")
    grp = lax.axis_index("grp")

    barrier = pltpu.get_barrier_semaphore()
    lines = (1, 2, 3, 4, 8, 12, 16, 20, 24, 28, 32)
    for k in range(1, GRP):
        pl.semaphore_signal(
            barrier, inc=1, device_id=(stn, lax.rem(grp + k, GRP)), device_id_type=MESH
        )
    for k in lines:
        pl.semaphore_signal(
            barrier, inc=1, device_id=(partner(stn, k), grp), device_id_type=MESH
        )

    def load(i):
        source, target = ((short_hbm, short), (second_hbm, second), (pick_hbm, pick))[i]
        return pltpu.make_async_copy(source, target, table_sem.at[i])

    for i in range(3):
        load(i).start()

    def widen_own(i, _):
        v = x_ref[i // 16, lax.rem(i, 16)].astype(F32)
        ext[TILES + i] = v[:8]
        ext[TILES + HALF + i] = v[8:]
        return 0

    lax.fori_loop(0, HALF, widen_own, 0, unroll=8)

    step = 8

    def short_filter(i, _):
        for a in range(2):
            taps = [
                jnp.broadcast_to(beam_taps[pl.ds(k, 1), a * LANES : (a + 1) * LANES], (8, LANES))
                for k in range(TAPS)
            ]
            base = TILES + i * (2 * step) + a
            window = [ext[base + 2 * j] for j in range(1 - TAPS, step)]
            for f in range(step):
                total = window[f + TAPS - 1] * taps[0]
                for k in range(1, TAPS):
                    total = total + window[f + TAPS - 1 - k] * taps[k]
                fs[a, pl.ds(pl.multiple_of((i * step + f) * 8, 8), 8), :] = total
        return 0

    def short_spectra(first_frame, frames, target):
        lanes = target.shape[-1]
        halves = []
        for st in range(2):
            for p in range(2):
                for part in range(2):
                    for a in range(2):
                        z_ref[pl.ds(p * frames, frames), pl.ds(part * 256 + a * LANES, LANES)] = fs[
                            a, pl.ds(first_frame * 8 + part * 4 + st * 2 + p, frames, stride=8), :
                        ].astype(BF)
            if lanes > 2 * frames:
                z_ref[pl.ds(2 * frames, lanes - 2 * frames), :] = jnp.zeros(
                    (lanes - 2 * frames, 512), BF
                )
            halves.append(dot_t(short[...], z_ref[pl.ds(0, lanes), :]).reshape(STN, 8, lanes))
        target[...] = jnp.concatenate(halves, axis=1).astype(BF)

    lax.fori_loop(FRAMES_B // step, SHORT_FRAMES // step, short_filter, 0)

    pl.semaphore_wait(barrier, len(lines) + GRP - 1)

    def halo(c):
        return pltpu.make_async_remote_copy(
            src_ref=x_ref.at[:, pl.ds(4 * c, 4)],
            dst_ref=hist.at[:, pl.ds(4 * c, 4)],
            send_sem=halo_send.at[c],
            recv_sem=halo_recv.at[c],
            device_id=(stn, lax.rem(grp + 1, GRP)),
            device_id_type=MESH,
        )

    @pl.when(grp < GRP - 1)
    def _():
        for c in range(4):
            halo(c).start()

    for k in (1, 2, 3):
        pl.semaphore_signal(row_sem, inc=1, device_id=(partner(stn, k), grp), device_id_type=MESH)

    load(0).wait()
    short_spectra(FRAMES_B, FRAMES_A, send_a)

    pl.semaphore_wait(row_sem, 3)
    pl.semaphore_signal(column_sem, inc=1, device_id=(partner(stn, 32), grp), device_id_type=MESH)
    pl.semaphore_wait(column_sem, 1)

    def exchange(source, target, send_sem, recv_sem, k):
        other = partner(stn, k)
        return pltpu.make_async_remote_copy(
            src_ref=source.at[other],
            dst_ref=target.at[stn],
            send_sem=send_sem,
            recv_sem=recv_sem,
            device_id=(other, grp),
            device_id_type=MESH,
        )

    def send_all(source, target, send_sem, recv_sem):
        def body(k, _):
            exchange(source, target, send_sem, recv_sem, k).start()
            return 0

        lax.fori_loop(1, STN, body, 0)
        target[stn] = source[stn]

    def wait_all(source, target, send_sem, recv_sem):
        span = pl.ds(0, STN - 1)
        pltpu.make_async_copy(source.at[span], target.at[span], recv_sem).wait()

    def wait_sent(source, target, send_sem, recv_sem):
        span = pl.ds(0, STN - 1)
        pltpu.make_async_copy(source.at[span], target.at[span], send_sem).wait()

    a_args = (send_a, recv_a, a_send_sem, a_recv_sem)
    b_args = (send_b, recv_b, b_send_sem, b_recv_sem)
    spec_args = (send_spec, recv_spec, spec_send_sem, spec_recv_sem)
    send_all(*a_args)

    @pl.when(grp == 0)
    def _():
        def clear(i, _):
            ext[i] = jnp.zeros((8, LANES), F32)
            return 0

        lax.fori_loop(0, TILES, clear, 0, unroll=8)

    for c in range(4):

        @pl.when(grp > 0)
        def _(c=c):
            halo(c).wait_recv()

            def body(i, _):
                for j in range(4 * c, 4 * c + 4):
                    v = hist[i, j].astype(F32)
                    ext[i * 16 + j] = v[:8]
                    ext[HALF + i * 16 + j] = v[8:]
                return 0

            lax.fori_loop(0, FRAMES, body, 0)

        def long_filter(j, _, c=c):
            i = 4 * c + lax.rem(j, 4) + 16 * (j // 4)
            taps = [
                jnp.broadcast_to(
                    corr_taps[pl.ds(k, 1), pl.ds(pl.multiple_of(i * LANES, LANES), LANES)], (8, LANES)
                )
                for k in range(TAPS)
            ]
            window = [ext[i + 32 * m] for m in range(2 * FRAMES)]
            for g in range(FRAMES):
                total = window[g + TAPS - 1] * taps[0]
                for k in range(1, TAPS):
                    total = total + window[g + TAPS - 1 - k] * taps[k]
                fl[pl.ds(pl.multiple_of((g * 32 + i) * 8, 8), 8), :] = total
            return 0

        lax.fori_loop(0, 8, long_filter, 0)

    low = lax.broadcasted_iota(jnp.int32, (32, LANES), 1) < RADIX

    def first_factor(g, _):
        rows = []
        for part in range(2):
            even, odd = [], []
            for q2 in range(2):
                a = fl[pl.ds(g * 256 + part * 4 + 2 * q2, 32, stride=8), :]
                b = fl[pl.ds(g * 256 + part * 4 + 2 * q2 + 1, 32, stride=8), :]
                even.append(jnp.where(low, a, pltpu.roll(b, RADIX, 1)))
                odd.append(jnp.where(low, pltpu.roll(a, RADIX, 1), b))
            rows.append(jnp.concatenate(even, axis=1))
            rows.append(jnp.concatenate(odd, axis=1))
        out = dot(first[...], jnp.concatenate(rows, axis=0).astype(BF))
        real, imag = out[:RADIX], out[RADIX:]
        at = pl.ds(pl.multiple_of(g * RADIX, RADIX), RADIX)
        tw[at, 0:256] = (real * twist[0] + imag * twist[1]).astype(BF)
        tw[at, 256:512] = (imag * twist[0] - real * twist[1]).astype(BF)
        return 0

    lax.fori_loop(0, FRAMES, first_factor, 0)
    tw[FRAMES * RADIX : 12 * RADIX, :] = jnp.zeros((RADIX, 512), BF)

    load(1).wait()
    for gpp in range(3):
        pairs = [
            dot_t(second[...], tw[(2 * gpp + e) * LANES : (2 * gpp + e + 1) * LANES, :]).reshape(STN, 8, LANES)
            for e in range(2)
        ]
        send_spec[:, 16 * gpp : 16 * gpp + 16, :] = jnp.concatenate(pairs, axis=1).astype(BF)
    send_all(*spec_args)

    lax.fori_loop(0, FRAMES_B // step, short_filter, 0)
    short_spectra(0, FRAMES_B, send_b)
    send_all(*b_args)

    shape = (256, 1024)
    column = lax.broadcasted_iota(jnp.int32, shape, 1)
    match = lax.broadcasted_iota(jnp.int32, shape, 0) == stn * 4 + (column // 2) % 4
    own_re = jnp.where(match & (column % 2 == 0), 1.0, 0.0).astype(BF)
    own_im = jnp.where(match & (column % 2 == 1), 1.0, 0.0).astype(BF)
    factor = 1.0 / math.sqrt(2 * STN)
    cos = (jnp.cos(angles[...]) * factor).astype(BF)
    sin = (jnp.sin(angles[...]) * factor).astype(BF)
    table[0] = dot(cos, own_re) - dot(sin, own_im)
    table[1] = dot(sin, own_re) + dot(cos, own_im)
    shape = (128, 1024)
    spread = jnp.where(
        lax.broadcasted_iota(jnp.int32, shape, 0) == lax.broadcasted_iota(jnp.int32, shape, 1) // 8,
        1.0,
        0.0,
    ).astype(BF)
    chosen = dot(index[...].astype(F32).astype(BF), spread)

    def choose(t, carry):
        real, imag = carry
        hit = chosen == t.astype(F32)
        return (
            jnp.where(hit, jnp.broadcast_to(table[0, pl.ds(t, 1), :], (16, 1024)), real),
            jnp.where(hit, jnp.broadcast_to(table[1, pl.ds(t, 1), :], (16, 1024)), imag),
        )

    zero = jnp.zeros((16, 1024), F32)
    chosen_parts = lax.fori_loop(0, 64, choose, (zero, zero))
    channel = (lax.broadcasted_iota(jnp.int32, (16, 1024), 1) // 2) % 4
    for po in range(2):
        for ci in range(4):
            weights[po * 64 + ci * 16 : po * 64 + ci * 16 + 16, :] = jnp.where(
                channel == ci, chosen_parts[po], 0.0
            ).astype(BF)

    def beam_power(source):
        fields = dot(weights[...], source[...].reshape(1024, source.shape[-1]))
        return fields[:64] * fields[:64] + fields[64:] * fields[64:]

    wait_all(*a_args)
    power = beam_power(recv_a)
    power_ref[:, FRAMES_B:SHORT_FRAMES] = power[:, :FRAMES_A] + power[:, FRAMES_A:]

    load(2).wait()
    wait_all(*spec_args)

    def gather_rows(b, _):
        for gpp in range(3):
            block = recv_spec[pl.ds(b * 16, 16), 16 * gpp : 16 * gpp + 16, :].reshape(256, LANES)
            rows = dot(pick[...], block).astype(BF)
            for e in range(2):
                at = 384 * e
                lanes = (2 * gpp + e) * LANES
                wide = pl.ds(pl.multiple_of(b * 128, 128), 128)
                narrow = pl.ds(pl.multiple_of(b * 64, 64), 64)
                lhs[wide, lanes : lanes + LANES] = rows[at : at + 128]
                lhs[wide, 768 + lanes : 768 + lanes + LANES] = rows[at + 128 : at + 256]
                rhs[narrow, lanes : lanes + LANES] = rows[at + 256 : at + 320]
                rhs[narrow, 768 + lanes : 768 + lanes + LANES] = rows[at + 320 : at + 384]
        return 0

    lax.fori_loop(0, 4, gather_rows, 0)
    for i in range(GRP):
        partial = dot_t(lhs[i * 128 : i * 128 + 128, :], rhs[...])
        part_own[i] = partial
        part_send[i] = partial.astype(BF)

    def hand_over(k):
        other = lax.rem(grp + k, GRP)
        return pltpu.make_async_remote_copy(
            src_ref=part_send.at[other],
            dst_ref=part_recv.at[k - 1],
            send_sem=part_send_sem.at[k - 1],
            recv_sem=part_recv_sem.at[k - 1],
            device_id=(stn, other),
            device_id_type=MESH,
        )

    for k in range(1, GRP):
        hand_over(k).start()

    wait_all(*b_args)
    power = beam_power(recv_b)
    power_ref[:, 0:FRAMES_B] = power[:, :FRAMES_B] + power[:, FRAMES_B : 2 * FRAMES_B]

    total = part_own[grp]
    for k in range(1, GRP):
        hand_over(k).wait_recv()
        total = total + part_recv[k - 1].astype(F32)
    vis_ref[...] = total * (1.0 / math.sqrt(4 * FRAMES * RADIX))

    for k in range(1, GRP):
        hand_over(k).wait_send()
    wait_sent(*a_args)
    wait_sent(*spec_args)
    wait_sent(*b_args)

    @pl.when(grp < GRP - 1)
    def _():
        for c in range(4):
            halo(c).wait_send()


def on_device(voltages, corr_taps, beam_taps, angle_table, table_index):
    x = voltages.reshape(8, 2, HALF, LANES).transpose(2, 1, 0, 3).reshape(FRAMES, 16, 16, LANES)
    tables = [jnp.asarray(t) for t in constant_tables()]
    vmem = pl.BlockSpec(memory_space=pltpu.VMEM)
    dma = pltpu.SemaphoreType.DMA
    vis, power = pl.pallas_call(
        kernel,
        out_shape=(
            jax.ShapeDtypeStruct((128, 256), F32),
            jax.ShapeDtypeStruct((64, SHORT_FRAMES), F32),
        ),
        in_specs=[vmem] * 7 + [pl.BlockSpec(memory_space=pl.ANY)] * 3,
        out_specs=(vmem, vmem),
        scratch_shapes=[
            pltpu.VMEM((512, 512), BF),
            pltpu.VMEM((512, 512), BF),
            pltpu.VMEM((768, 256), BF),
            pltpu.VMEM((FRAMES, 16, 16, LANES), BF),
            pltpu.VMEM((2 * TILES, 8, LANES), F32),
            pltpu.VMEM((2, SHORT_FRAMES * 8, LANES), F32),
            pltpu.VMEM((FRAMES * 256, LANES), F32),
            pltpu.VMEM((256, 512), BF),
            pltpu.VMEM((12 * RADIX, 512), BF),
            pltpu.VMEM((STN, 16, 256), BF),
            pltpu.VMEM((STN, 16, 256), BF),
            pltpu.VMEM((STN, 16, LANES), BF),
            pltpu.VMEM((STN, 16, LANES), BF),
            pltpu.VMEM((STN, 48, LANES), BF),
            pltpu.VMEM((STN, 48, LANES), BF),
            pltpu.VMEM((2, 64, 1024), F32),
            pltpu.VMEM((128, 1024), BF),
            pltpu.VMEM((512, 1536), BF),
            pltpu.VMEM((256, 1536), BF),
            pltpu.VMEM((GRP, 128, 256), F32),
            pltpu.VMEM((GRP, 128, 256), BF),
            pltpu.VMEM((GRP - 1, 128, 256), BF),
            pltpu.SemaphoreType.REGULAR,
            pltpu.SemaphoreType.REGULAR,
            dma((3,)),
            dma((4,)),
            dma((4,)),
            dma,
            dma,
            dma,
            dma,
            dma,
            dma,
            dma((GRP - 1,)),
            dma((GRP - 1,)),
        ],
        compiler_params=pltpu.CompilerParams(
            collective_id=0, has_side_effects=True, vmem_limit_bytes=48 * 1024 * 1024
        ),
    )(x, corr_taps, beam_taps, angle_table, table_index, *tables)
    return vis.reshape(1, 64, 2, 256), power.reshape(4, 16, SHORT_FRAMES)


def solution(mesh):
    in_specs = (P(None, "stn", None, "grp"), P(), P(), P(), P())
    out_specs = (P("stn", "grp", None, None), P("stn", None, "grp"))
    return jax.shard_map(
        on_device, mesh=mesh, in_specs=in_specs, out_specs=out_specs, check_vma=False
    )
```

```python
import functools
import math

import jax
import jax.numpy as jnp
import ml_dtypes
import numpy as np
from jax import lax
from jax.experimental import pallas as pl
from jax.experimental.pallas import tpu as pltpu
from jax.sharding import PartitionSpec as P

MESH = pl.DeviceIdType.MESH
BF = jnp.bfloat16
F32 = jnp.float32

RADIX = 64
TAPS = 12
STN = 64
GRP = 4
LANES = 128
TILES = 352
HALF = 176
FRAMES = 11
SHORT_FRAMES = 176
FRAMES_B = 48
GROUPS = ((8, 3), (4, 4), (0, 4))
FRAMES_A = SHORT_FRAMES - FRAMES_B


def dft_tables(length):
    k = np.arange(length)
    phases = (k[:, None] * k[None, :] % length) * (2.0 * math.pi / length)
    factor = 1.0 / math.sqrt(length)
    return np.cos(phases) * factor, np.sin(phases) * factor


def constant_tables():
    bf = ml_dtypes.bfloat16
    cos, sin = dft_tables(RADIX)
    order = np.concatenate([np.arange(0, RADIX, 2), np.arange(1, RADIX, 2)])
    c, s = cos[order].T, sin[order].T
    first = np.block([[c, s], [-s, c]])
    k = np.arange(RADIX)
    phases = (k[:, None] * k[None, :]) * (2.0 * math.pi / (RADIX * RADIX))
    twist = np.stack([np.tile(np.cos(phases), (1, 4)), np.tile(np.sin(phases), (1, 4))])
    second = np.zeros((RADIX, 4, 2, 2, 4, RADIX))
    for q in range(4):
        second[:, q, 0, 0, q] = cos.T
        second[:, q, 0, 1, q] = sin.T
        second[:, q, 1, 0, q] = -sin.T
        second[:, q, 1, 1, q] = cos.T
    second = second.reshape(512, 512)
    cos, sin = dft_tables(256)
    short = np.zeros((256, 2, 2, 256))
    short[:, 0, 0] = cos.T
    short[:, 0, 1] = sin.T
    short[:, 1, 0] = -sin.T
    short[:, 1, 1] = cos.T
    short = short.reshape(512, 512)
    pick = np.zeros((2, 384, 16, 2, 4, 2))
    for pair in range(2):
        for src in range(16):
            for q in range(4):
                u = src * 4 + q
                pick[pair, 2 * u, src, pair, q, 0] = 1
                pick[pair, 2 * u + 1, src, pair, q, 1] = 1
                pick[pair, 128 + 2 * u, src, pair, q, 1] = 1
                pick[pair, 128 + 2 * u + 1, src, pair, q, 0] = -1
                pick[pair, 256 + u, src, pair, q, 0] = 1
                pick[pair, 320 + u, src, pair, q, 1] = 1
    pick = pick.reshape(768, 256)
    return (
        first.astype(bf),
        twist.astype(np.float32),
        second.astype(bf),
        short.astype(bf),
        pick.astype(bf),
    )


def dot(a, b):
    return lax.dot_general(a, b, (((1,), (0,)), ((), ())), preferred_element_type=F32)


def dot_t(a, b):
    return lax.dot_general(a, b, (((1,), (1,)), ((), ())), preferred_element_type=F32)


def partner(stn, offset):
    y = lax.rem(stn // 32 + offset // 32, 2)
    z = lax.rem(lax.rem(stn // 4, 8) + lax.rem(offset // 4, 8), 8)
    x = lax.rem(lax.rem(stn, 4) + lax.rem(offset, 4), 4)
    return y * 32 + z * 4 + x


def kernel(
    x_ref, corr_taps, beam_taps, angles, index, first, twist, second_hbm, short_hbm, pick_hbm,
    vis_ref, power_ref,
    second, short, pick,
    hist, ext, fs, fl, z_ref, tw, send_a, recv_a, send_b, recv_b, send_spec, recv_spec,
    table, weights, lhs, rhs, part_own, part_send, part_recv,
    row_sem, column_sem, table_sem, halo_send, halo_recv,
    a_send_sem, a_recv_sem, b_send_sem, b_recv_sem, spec_send_sem, spec_recv_sem,
    part_send_sem, part_recv_sem,
):
    stn = lax.axis_index("stn")
    grp = lax.axis_index("grp")

    barrier = pltpu.get_barrier_semaphore()
    lines = (1, 2, 3, 4, 8, 12, 16, 20, 24, 28, 32)
    for k in range(1, GRP):
        pl.semaphore_signal(
            barrier, inc=1, device_id=(stn, lax.rem(grp + k, GRP)), device_id_type=MESH
        )
    for k in lines:
        pl.semaphore_signal(
            barrier, inc=1, device_id=(partner(stn, k), grp), device_id_type=MESH
        )

    def load(i):
        source, target = ((short_hbm, short), (second_hbm, second), (pick_hbm, pick))[i]
        return pltpu.make_async_copy(source, target, table_sem.at[i])

    for i in range(3):
        load(i).start()

    def widen_own(i, _):
        v = x_ref[i].astype(F32)
        ext[TILES + 2 * i] = v[:8]
        ext[TILES + 2 * i + 1] = v[8:]
        return 0

    lax.fori_loop(0, HALF, widen_own, 0, unroll=8)

    step = 8

    def short_filter(i, _):
        for a in range(2):
            taps = [
                jnp.broadcast_to(beam_taps[pl.ds(k, 1), a * LANES : (a + 1) * LANES], (8, LANES))
                for k in range(TAPS)
            ]
            base = TILES + i * (2 * step) + a
            window = [ext[base + 2 * j] for j in range(1 - TAPS, step)]
            for f in range(step):
                total = window[f + TAPS - 1] * taps[0]
                for k in range(1, TAPS):
                    total = total + window[f + TAPS - 1 - k] * taps[k]
                fs[a, pl.ds(pl.multiple_of((i * step + f) * 8, 8), 8), :] = total
        return 0

    def short_spectra(first_frame, frames, target):
        lanes = target.shape[-1]
        halves = []
        for st in range(2):
            for p in range(2):
                for part in range(2):
                    for a in range(2):
                        z_ref[pl.ds(p * frames, frames), pl.ds(part * 256 + a * LANES, LANES)] = fs[
                            a, pl.ds(first_frame * 8 + part * 4 + st * 2 + p, frames, stride=8), :
                        ].astype(BF)
            if lanes > 2 * frames:
                z_ref[pl.ds(2 * frames, lanes - 2 * frames), :] = jnp.zeros(
                    (lanes - 2 * frames, 512), BF
                )
            halves.append(dot_t(short[...], z_ref[pl.ds(0, lanes), :]).reshape(STN, 8, lanes))
        target[...] = jnp.concatenate(halves, axis=1).astype(BF)

    lax.fori_loop(FRAMES_B // step, SHORT_FRAMES // step, short_filter, 0)
    load(0).wait()
    short_spectra(FRAMES_B, FRAMES_A, send_a)

    @pl.when(grp == 0)
    def _():
        def clear(i, _):
            ext[i] = jnp.zeros((8, LANES), F32)
            return 0

        lax.fori_loop(0, TILES, clear, 0, unroll=8)

    pl.semaphore_wait(barrier, len(lines) + GRP - 1)

    for k in (1, 2, 3):
        pl.semaphore_signal(row_sem, inc=1, device_id=(partner(stn, k), grp), device_id_type=MESH)

    def halo(c):
        first_frame, frames = GROUPS[c]
        at = pl.ds(16 * first_frame, 16 * frames)
        return pltpu.make_async_remote_copy(
            src_ref=x_ref.at[at],
            dst_ref=hist.at[at],
            send_sem=halo_send.at[c],
            recv_sem=halo_recv.at[c],
            device_id=(stn, lax.rem(grp + 1, GRP)),
            device_id_type=MESH,
        )

    @pl.when(grp < GRP - 1)
    def _():
        for c in range(3):
            halo(c).start()

    def exchange(source, target, send_sem, recv_sem, k):
        other = partner(stn, k)
        return pltpu.make_async_remote_copy(
            src_ref=source.at[other],
            dst_ref=target.at[stn],
            send_sem=send_sem,
            recv_sem=recv_sem,
            device_id=(other, grp),
            device_id_type=MESH,
        )

    def send_all(source, target, send_sem, recv_sem, start=1, stop=STN):
        def body(k, _):
            exchange(source, target, send_sem, recv_sem, k).start()
            return 0

        lax.fori_loop(start, stop, body, 0)
        if start == 1:
            target[stn] = source[stn]

    def wait_all(source, target, send_sem, recv_sem):
        span = pl.ds(0, STN - 1)
        pltpu.make_async_copy(source.at[span], target.at[span], recv_sem).wait()

    def wait_sent(source, target, send_sem, recv_sem):
        span = pl.ds(0, STN - 1)
        pltpu.make_async_copy(source.at[span], target.at[span], send_sem).wait()

    a_args = (send_a, recv_a, a_send_sem, a_recv_sem)
    b_args = (send_b, recv_b, b_send_sem, b_recv_sem)
    spec_args = [
        (send_spec.at[c], recv_spec.at[c], spec_send_sem.at[c], spec_recv_sem.at[c]) for c in range(3)
    ]

    pl.semaphore_wait(row_sem, 3)
    pl.semaphore_signal(column_sem, inc=1, device_id=(partner(stn, 32), grp), device_id_type=MESH)
    send_all(*a_args, 1, STN // 2)
    pl.semaphore_wait(column_sem, 1)
    send_all(*a_args, STN // 2, STN)

    low = lax.broadcasted_iota(jnp.int32, (32, LANES), 1) < RADIX
    tw[FRAMES * RADIX : 12 * RADIX, :] = jnp.zeros((RADIX, 512), BF)

    for c, (first_frame, frames) in enumerate(GROUPS):

        @pl.when(grp > 0)
        def _(c=c, first_frame=first_frame, frames=frames):
            halo(c).wait_recv()

            def body(i, _):
                v = hist[i].astype(F32)
                ext[2 * i] = v[:8]
                ext[2 * i + 1] = v[8:]
                return 0

            lax.fori_loop(16 * first_frame, 16 * (first_frame + frames), body, 0, unroll=8)

        def long_filter(i, _, first_frame=first_frame, frames=frames):
            taps = [
                jnp.broadcast_to(
                    corr_taps[pl.ds(k, 1), pl.ds(pl.multiple_of(i * LANES, LANES), LANES)], (8, LANES)
                )
                for k in range(TAPS)
            ]
            window = [ext[i + 32 * (first_frame + m)] for m in range(frames + TAPS - 1)]
            for g in range(frames):
                total = window[g + TAPS - 1] * taps[0]
                for k in range(1, TAPS):
                    total = total + window[g + TAPS - 1 - k] * taps[k]
                fl[pl.ds(pl.multiple_of(((first_frame + g) * 32 + i) * 8, 8), 8), :] = total
            return 0

        lax.fori_loop(0, 32, long_filter, 0)

        def first_factor(g, _):
            rows = []
            for part in range(2):
                even, odd = [], []
                for q2 in range(2):
                    a = fl[pl.ds(g * 256 + part * 4 + 2 * q2, 32, stride=8), :]
                    b = fl[pl.ds(g * 256 + part * 4 + 2 * q2 + 1, 32, stride=8), :]
                    even.append(jnp.where(low, a, pltpu.roll(b, RADIX, 1)))
                    odd.append(jnp.where(low, pltpu.roll(a, RADIX, 1), b))
                rows.append(jnp.concatenate(even, axis=1))
                rows.append(jnp.concatenate(odd, axis=1))
            out = dot(first[...], jnp.concatenate(rows, axis=0).astype(BF))
            real, imag = out[:RADIX], out[RADIX:]
            at = pl.ds(pl.multiple_of(g * RADIX, RADIX), RADIX)
            tw[at, 0:256] = (real * twist[0] + imag * twist[1]).astype(BF)
            tw[at, 256:512] = (imag * twist[0] - real * twist[1]).astype(BF)
            return 0

        lax.fori_loop(first_frame, first_frame + frames, first_factor, 0)

        if c == 0:
            load(1).wait()
        pairs = [
            dot_t(second[...], tw[at : at + LANES, :]).reshape(STN, 8, LANES)
            for at in (first_frame * RADIX, first_frame * RADIX + LANES)
        ]
        send_spec[c] = jnp.concatenate(pairs, axis=1).astype(BF)
        send_all(*spec_args[c])

    lax.fori_loop(0, FRAMES_B // step, short_filter, 0)
    short_spectra(0, FRAMES_B, send_b)
    send_all(*b_args)

    shape = (256, 1024)
    column = lax.broadcasted_iota(jnp.int32, shape, 1)
    match = lax.broadcasted_iota(jnp.int32, shape, 0) == stn * 4 + (column // 2) % 4
    own_re = jnp.where(match & (column % 2 == 0), 1.0, 0.0).astype(BF)
    own_im = jnp.where(match & (column % 2 == 1), 1.0, 0.0).astype(BF)
    factor = 1.0 / math.sqrt(2 * STN)
    cos = (jnp.cos(angles[...]) * factor).astype(BF)
    sin = (jnp.sin(angles[...]) * factor).astype(BF)
    table[0] = dot(cos, own_re) - dot(sin, own_im)
    table[1] = dot(sin, own_re) + dot(cos, own_im)
    shape = (128, 1024)
    spread = jnp.where(
        lax.broadcasted_iota(jnp.int32, shape, 0) == lax.broadcasted_iota(jnp.int32, shape, 1) // 8,
        1.0,
        0.0,
    ).astype(BF)
    chosen = dot(index[...].astype(F32).astype(BF), spread)

    def choose(t, carry):
        real, imag = carry
        hit = chosen == t.astype(F32)
        return (
            jnp.where(hit, jnp.broadcast_to(table[0, pl.ds(t, 1), :], (16, 1024)), real),
            jnp.where(hit, jnp.broadcast_to(table[1, pl.ds(t, 1), :], (16, 1024)), imag),
        )

    zero = jnp.zeros((16, 1024), F32)
    chosen_parts = lax.fori_loop(0, 64, choose, (zero, zero))
    channel = (lax.broadcasted_iota(jnp.int32, (16, 1024), 1) // 2) % 4
    for po in range(2):
        for ci in range(4):
            weights[po * 64 + ci * 16 : po * 64 + ci * 16 + 16, :] = jnp.where(
                channel == ci, chosen_parts[po], 0.0
            ).astype(BF)

    def beam_power(source):
        fields = dot(weights[...], source[...].reshape(1024, source.shape[-1]))
        return fields[:64] * fields[:64] + fields[64:] * fields[64:]

    wait_all(*a_args)
    power = beam_power(recv_a)
    power_ref[:, FRAMES_B:SHORT_FRAMES] = power[:, :FRAMES_A] + power[:, FRAMES_A:]

    def hand_over(k):
        other = lax.rem(grp + k, GRP)
        return pltpu.make_async_remote_copy(
            src_ref=part_send.at[other],
            dst_ref=part_recv.at[k - 1],
            send_sem=part_send_sem.at[k - 1],
            recv_sem=part_recv_sem.at[k - 1],
            device_id=(stn, other),
            device_id_type=MESH,
        )

    load(2).wait()
    for c in range(3):
        wait_all(*spec_args[c])

        def gather_rows(b, _, c=c):
            block = recv_spec[c, pl.ds(b * 16, 16)].reshape(256, LANES)
            rows = dot(pick[...], block).astype(BF)
            wide = pl.ds(pl.multiple_of(b * 128, 128), 128)
            narrow = pl.ds(pl.multiple_of(b * 64, 64), 64)
            for e in range(2):
                at = 384 * e
                lanes = 2 * e * LANES
                lhs[wide, lanes : lanes + LANES] = rows[at : at + 128]
                lhs[wide, lanes + LANES : lanes + 2 * LANES] = rows[at + 128 : at + 256]
                rhs[narrow, lanes : lanes + LANES] = rows[at + 256 : at + 320]
                rhs[narrow, lanes + LANES : lanes + 2 * LANES] = rows[at + 320 : at + 384]
            return 0

        lax.fori_loop(0, 4, gather_rows, 0)
        for k in (1, 2, 3, 0):
            owner = lax.rem(grp + k, GRP)
            partial = dot_t(lhs[pl.ds(pl.multiple_of(owner * 128, 128), 128), :], rhs[...])
            if c > 0:
                partial = partial + part_own[k]
            if c < 2 or k == 0:
                part_own[k] = partial
            else:
                part_send[owner] = partial.astype(BF)
                hand_over(k).start()

    wait_all(*b_args)
    power = beam_power(recv_b)
    power_ref[:, 0:FRAMES_B] = power[:, :FRAMES_B] + power[:, FRAMES_B : 2 * FRAMES_B]

    total = part_own[0]
    for k in range(1, GRP):
        hand_over(k).wait_recv()
        total = total + part_recv[k - 1].astype(F32)
    vis_ref[...] = total * (1.0 / math.sqrt(4 * FRAMES * RADIX))

    for k in range(1, GRP):
        hand_over(k).wait_send()
    wait_sent(*a_args)
    for c in range(3):
        wait_sent(*spec_args[c])
    wait_sent(*b_args)

    @pl.when(grp < GRP - 1)
    def _():
        for c in range(3):
            halo(c).wait_send()


def on_device(voltages, corr_taps, beam_taps, angle_table, table_index):
    x = voltages.reshape(8, TILES, LANES).transpose(1, 0, 2).reshape(HALF, 16, LANES)
    tables = [jnp.asarray(t) for t in constant_tables()]
    vmem = pl.BlockSpec(memory_space=pltpu.VMEM)
    dma = pltpu.SemaphoreType.DMA
    vis, power = pl.pallas_call(
        kernel,
        out_shape=(
            jax.ShapeDtypeStruct((128, 256), F32),
            jax.ShapeDtypeStruct((64, SHORT_FRAMES), F32),
        ),
        in_specs=[vmem] * 7 + [pl.BlockSpec(memory_space=pltpu.HBM)] * 3,
        out_specs=(vmem, vmem),
        scratch_shapes=[
            pltpu.VMEM((512, 512), BF),
            pltpu.VMEM((512, 512), BF),
            pltpu.VMEM((768, 256), BF),
            pltpu.VMEM((HALF, 16, LANES), BF),
            pltpu.VMEM((2 * TILES, 8, LANES), F32),
            pltpu.VMEM((2, SHORT_FRAMES * 8, LANES), F32),
            pltpu.VMEM((FRAMES * 256, LANES), F32),
            pltpu.VMEM((256, 512), BF),
            pltpu.VMEM((12 * RADIX, 512), BF),
            pltpu.VMEM((STN, 16, 256), BF),
            pltpu.VMEM((STN, 16, 256), BF),
            pltpu.VMEM((STN, 16, LANES), BF),
            pltpu.VMEM((STN, 16, LANES), BF),
            pltpu.VMEM((3, STN, 16, LANES), BF),
            pltpu.VMEM((3, STN, 16, LANES), BF),
            pltpu.VMEM((2, 64, 1024), F32),
            pltpu.VMEM((128, 1024), BF),
            pltpu.VMEM((512, 512), BF),
            pltpu.VMEM((256, 512), BF),
            pltpu.VMEM((GRP, 128, 256), F32),
            pltpu.VMEM((GRP, 128, 256), BF),
            pltpu.VMEM((GRP - 1, 128, 256), BF),
            pltpu.SemaphoreType.REGULAR,
            pltpu.SemaphoreType.REGULAR,
            dma((3,)),
            dma((3,)),
            dma((3,)),
            dma,
            dma,
            dma,
            dma,
            dma((3,)),
            dma((3,)),
            dma((GRP - 1,)),
            dma((GRP - 1,)),
        ],
        compiler_params=pltpu.CompilerParams(
            collective_id=0, has_side_effects=True, vmem_limit_bytes=48 * 1024 * 1024
        ),
    )(x, corr_taps, beam_taps, angle_table, table_index, *tables)
    return vis.reshape(1, 64, 2, 256), power.reshape(4, 16, SHORT_FRAMES)


def solution(mesh):
    in_specs = (P(None, "stn", None, "grp"), P(), P(), P(), P())
    out_specs = (P("stn", "grp", None, None), P("stn", None, "grp"))
    return jax.shard_map(
        on_device, mesh=mesh, in_specs=in_specs, out_specs=out_specs, check_vma=False
    )
```

```python
import functools
import math

import jax
import jax.numpy as jnp
import ml_dtypes
import numpy as np
from jax import lax
from jax.experimental import pallas as pl
from jax.experimental.pallas import tpu as pltpu
from jax.sharding import PartitionSpec as P

MESH = pl.DeviceIdType.MESH
BF = jnp.bfloat16
F32 = jnp.float32

RADIX = 64
TAPS = 12
STN = 64
GRP = 4
LANES = 128
TILES = 352
HALF = 176
FRAMES = 11
SHORT_FRAMES = 176
LATE = 40
GROUPS = ((8, 3), (4, 4), (0, 4))
BEAM_GROUPS = ((112, 64), (48, 64), (0, 48))


def dft_tables(length):
    k = np.arange(length)
    phases = (k[:, None] * k[None, :] % length) * (2.0 * math.pi / length)
    factor = 1.0 / math.sqrt(length)
    return np.cos(phases) * factor, np.sin(phases) * factor


def constant_tables():
    bf = ml_dtypes.bfloat16
    cos, sin = dft_tables(RADIX)
    order = np.concatenate([np.arange(0, RADIX, 2), np.arange(1, RADIX, 2)])
    c, s = cos[order].T, sin[order].T
    first = np.block([[c, s], [-s, c]])
    k = np.arange(RADIX)
    phases = (k[:, None] * k[None, :]) * (2.0 * math.pi / (RADIX * RADIX))
    twist = np.stack([np.tile(np.cos(phases), (1, 4)), np.tile(np.sin(phases), (1, 4))])
    second = np.zeros((RADIX, 4, 2, 2, 4, RADIX))
    for q in range(4):
        second[:, q, 0, 0, q] = cos.T
        second[:, q, 0, 1, q] = sin.T
        second[:, q, 1, 0, q] = -sin.T
        second[:, q, 1, 1, q] = cos.T
    second = second.reshape(512, 512)
    cos, sin = dft_tables(256)
    short = np.zeros((256, 2, 2, 256))
    short[:, 0, 0] = cos.T
    short[:, 0, 1] = sin.T
    short[:, 1, 0] = -sin.T
    short[:, 1, 1] = cos.T
    short = short.reshape(512, 512)
    pick = np.zeros((2, 384, 16, 2, 4, 2))
    for pair in range(2):
        for src in range(16):
            for q in range(4):
                u = src * 4 + q
                pick[pair, 2 * u, src, pair, q, 0] = 1
                pick[pair, 2 * u + 1, src, pair, q, 1] = 1
                pick[pair, 128 + 2 * u, src, pair, q, 1] = 1
                pick[pair, 128 + 2 * u + 1, src, pair, q, 0] = -1
                pick[pair, 256 + u, src, pair, q, 0] = 1
                pick[pair, 320 + u, src, pair, q, 1] = 1
    pick = pick.reshape(768, 256)
    return (
        first.astype(bf),
        twist.astype(np.float32),
        second.astype(bf),
        short.astype(bf),
        pick.astype(bf),
    )


def dot(a, b):
    return lax.dot_general(a, b, (((1,), (0,)), ((), ())), preferred_element_type=F32)


def dot_t(a, b):
    return lax.dot_general(a, b, (((1,), (1,)), ((), ())), preferred_element_type=F32)


def partner(stn, offset):
    y = lax.rem(stn // 32 + offset // 32, 2)
    z = lax.rem(lax.rem(stn // 4, 8) + lax.rem(offset // 4, 8), 8)
    x = lax.rem(lax.rem(stn, 4) + lax.rem(offset, 4), 4)
    return y * 32 + z * 4 + x


def kernel(
    x_ref, corr_taps, beam_taps, angles, index, first, twist, second_hbm, short_hbm, pick_hbm,
    vis_ref, power_ref,
    second, short, pick,
    hist, ext, fs, fl, z_ref, tw, send_beam, recv_beam, send_spec, recv_spec,
    table, weights, lhs, rhs, part_own, part_send, part_recv,
    row_sem, column_sem, table_sem, halo_send, halo_recv,
    beam_send_sem, beam_recv_sem, spec_send_sem, spec_recv_sem, late_sem,
    part_send_sem, part_recv_sem,
):
    stn = lax.axis_index("stn")
    grp = lax.axis_index("grp")

    barrier = pltpu.get_barrier_semaphore()
    lines = (1, 2, 3, 4, 8, 12, 16, 20, 24, 28, 32)
    for k in range(1, GRP):
        pl.semaphore_signal(
            barrier, inc=1, device_id=(stn, lax.rem(grp + k, GRP)), device_id_type=MESH
        )
    for k in lines:
        pl.semaphore_signal(
            barrier, inc=1, device_id=(partner(stn, k), grp), device_id_type=MESH
        )

    def load(i):
        source, target = ((short_hbm, short), (second_hbm, second), (pick_hbm, pick))[i]
        return pltpu.make_async_copy(source, target, table_sem.at[i])

    for i in range(3):
        load(i).start()

    def widen_own(i, _):
        v = x_ref[i].astype(F32)
        ext[TILES + 2 * i] = v[:8]
        ext[TILES + 2 * i + 1] = v[8:]
        return 0

    lax.fori_loop(0, HALF, widen_own, 0, unroll=8)

    step = 8

    def short_filter(i, _):
        for a in range(2):
            taps = [
                jnp.broadcast_to(beam_taps[pl.ds(k, 1), a * LANES : (a + 1) * LANES], (8, LANES))
                for k in range(TAPS)
            ]
            base = TILES + i * (2 * step) + a
            window = [ext[base + 2 * j] for j in range(1 - TAPS, step)]
            for f in range(step):
                total = window[f + TAPS - 1] * taps[0]
                for k in range(1, TAPS):
                    total = total + window[f + TAPS - 1 - k] * taps[k]
                fs[a, pl.ds(pl.multiple_of((i * step + f) * 8, 8), 8), :] = total
        return 0

    def short_spectra(c):
        first_frame, frames = BEAM_GROUPS[c]
        lax.fori_loop(first_frame // step, (first_frame + frames) // step, short_filter, 0)
        halves = []
        for st in range(2):
            for p in range(2):
                for part in range(2):
                    for a in range(2):
                        z_ref[pl.ds(p * frames, frames), pl.ds(part * 256 + a * LANES, LANES)] = fs[
                            a, pl.ds(first_frame * 8 + part * 4 + st * 2 + p, frames, stride=8), :
                        ].astype(BF)
            if frames < 64:
                z_ref[pl.ds(2 * frames, LANES - 2 * frames), :] = jnp.zeros((LANES - 2 * frames, 512), BF)
            halves.append(dot_t(short[...], z_ref[...]).reshape(STN, 8, LANES))
        send_beam[c] = jnp.concatenate(halves, axis=1).astype(BF)

    load(0).wait()
    short_spectra(0)

    @pl.when(grp == 0)
    def _():
        def clear(i, _):
            ext[i] = jnp.zeros((8, LANES), F32)
            return 0

        lax.fori_loop(0, TILES, clear, 0, unroll=8)

    pl.semaphore_wait(barrier, len(lines) + GRP - 1)

    for k in (1, 2, 3):
        pl.semaphore_signal(row_sem, inc=1, device_id=(partner(stn, k), grp), device_id_type=MESH)

    def halo(c):
        first_frame, frames = GROUPS[c]
        at = pl.ds(16 * first_frame, 16 * frames)
        return pltpu.make_async_remote_copy(
            src_ref=x_ref.at[at],
            dst_ref=hist.at[at],
            send_sem=halo_send.at[c],
            recv_sem=halo_recv.at[c],
            device_id=(stn, lax.rem(grp + 1, GRP)),
            device_id_type=MESH,
        )

    def exchange(source, target, send_sem, recv_sem, k):
        other = partner(stn, k)
        return pltpu.make_async_remote_copy(
            src_ref=source.at[other],
            dst_ref=target.at[stn],
            send_sem=send_sem,
            recv_sem=recv_sem,
            device_id=(other, grp),
            device_id_type=MESH,
        )

    def send_all(source, target, send_sem, recv_sem, start=1, stop=STN):
        def body(k, _):
            exchange(source, target, send_sem, recv_sem, k).start()
            return 0

        lax.fori_loop(start, stop, body, 0)
        if start == 1:
            target[stn] = source[stn]

    def wait_all(source, target, send_sem, recv_sem):
        span = pl.ds(0, STN - 1)
        pltpu.make_async_copy(source.at[span], target.at[span], recv_sem).wait()

    def wait_sent(source, target, send_sem, recv_sem):
        span = pl.ds(0, STN - 1)
        pltpu.make_async_copy(source.at[span], target.at[span], send_sem).wait()

    beam_args = [
        (send_beam.at[c], recv_beam.at[c], beam_send_sem.at[c], beam_recv_sem.at[c]) for c in range(3)
    ]
    spec_args = [
        (send_spec.at[c], recv_spec.at[c], spec_send_sem.at[c], spec_recv_sem.at[c]) for c in range(3)
    ]

    for k in range(4, STN // 2, 4):
        exchange(*beam_args[0], k).start()
    recv_beam[0, stn] = send_beam[0, stn]

    @pl.when(grp < GRP - 1)
    def _():
        for c in range(3):
            halo(c).start()

    pl.semaphore_wait(row_sem, 3)
    pl.semaphore_signal(column_sem, inc=1, device_id=(partner(stn, 32), grp), device_id_type=MESH)

    def to_plane(k, _):
        exchange(*beam_args[0], k + 1 + k // 3).start()
        return 0

    lax.fori_loop(0, 24, to_plane, 0)
    short_spectra(1)
    send_all(*beam_args[1], 1, STN // 2)

    pl.semaphore_wait(column_sem, 1)
    send_all(*beam_args[0], STN // 2, STN)
    send_all(*beam_args[1], STN // 2, STN)

    low = lax.broadcasted_iota(jnp.int32, (32, LANES), 1) < RADIX
    tw[FRAMES * RADIX : 12 * RADIX, :] = jnp.zeros((RADIX, 512), BF)

    for c, (first_frame, frames) in enumerate(GROUPS):

        @pl.when(grp > 0)
        def _(c=c, first_frame=first_frame, frames=frames):
            halo(c).wait_recv()

            def body(i, _):
                v = hist[i].astype(F32)
                ext[2 * i] = v[:8]
                ext[2 * i + 1] = v[8:]
                return 0

            lax.fori_loop(16 * first_frame, 16 * (first_frame + frames), body, 0, unroll=8)

        def long_filter(i, _, first_frame=first_frame, frames=frames):
            taps = [
                jnp.broadcast_to(
                    corr_taps[pl.ds(k, 1), pl.ds(pl.multiple_of(i * LANES, LANES), LANES)], (8, LANES)
                )
                for k in range(TAPS)
            ]
            window = [ext[i + 32 * (first_frame + m)] for m in range(frames + TAPS - 1)]
            for g in range(frames):
                total = window[g + TAPS - 1] * taps[0]
                for k in range(1, TAPS):
                    total = total + window[g + TAPS - 1 - k] * taps[k]
                fl[pl.ds(pl.multiple_of(((first_frame + g) * 32 + i) * 8, 8), 8), :] = total
            return 0

        lax.fori_loop(0, 32, long_filter, 0)

        def first_factor(g, _):
            rows = []
            for part in range(2):
                even, odd = [], []
                for q2 in range(2):
                    a = fl[pl.ds(g * 256 + part * 4 + 2 * q2, 32, stride=8), :]
                    b = fl[pl.ds(g * 256 + part * 4 + 2 * q2 + 1, 32, stride=8), :]
                    even.append(jnp.where(low, a, pltpu.roll(b, RADIX, 1)))
                    odd.append(jnp.where(low, pltpu.roll(a, RADIX, 1), b))
                rows.append(jnp.concatenate(even, axis=1))
                rows.append(jnp.concatenate(odd, axis=1))
            out = dot(first[...], jnp.concatenate(rows, axis=0).astype(BF))
            real, imag = out[:RADIX], out[RADIX:]
            at = pl.ds(pl.multiple_of(g * RADIX, RADIX), RADIX)
            tw[at, 0:256] = (real * twist[0] + imag * twist[1]).astype(BF)
            tw[at, 256:512] = (imag * twist[0] - real * twist[1]).astype(BF)
            return 0

        lax.fori_loop(first_frame, first_frame + frames, first_factor, 0)

        if c == 0:
            load(1).wait()
        pairs = [
            dot_t(second[...], tw[at : at + LANES, :]).reshape(STN, 8, LANES)
            for at in (first_frame * RADIX, first_frame * RADIX + LANES)
        ]
        send_spec[c] = jnp.concatenate(pairs, axis=1).astype(BF)
        if c < 2:
            send_all(*spec_args[c])
        else:
            send_all(*spec_args[c], 1, LATE)
            send_all(send_spec.at[c], recv_spec.at[c], late_sem, spec_recv_sem.at[c], LATE, STN)

    short_spectra(2)

    shape = (256, 1024)
    column = lax.broadcasted_iota(jnp.int32, shape, 1)
    match = lax.broadcasted_iota(jnp.int32, shape, 0) == stn * 4 + (column // 2) % 4
    own_re = jnp.where(match & (column % 2 == 0), 1.0, 0.0).astype(BF)
    own_im = jnp.where(match & (column % 2 == 1), 1.0, 0.0).astype(BF)
    factor = 1.0 / math.sqrt(2 * STN)
    cos = (jnp.cos(angles[...]) * factor).astype(BF)
    sin = (jnp.sin(angles[...]) * factor).astype(BF)
    table[0] = dot(cos, own_re) - dot(sin, own_im)
    table[1] = dot(sin, own_re) + dot(cos, own_im)
    shape = (128, 1024)
    spread = jnp.where(
        lax.broadcasted_iota(jnp.int32, shape, 0) == lax.broadcasted_iota(jnp.int32, shape, 1) // 8,
        1.0,
        0.0,
    ).astype(BF)
    chosen = dot(index[...].astype(F32).astype(BF), spread)

    def choose(t, carry):
        real, imag = carry
        hit = chosen == t.astype(F32)
        return (
            jnp.where(hit, jnp.broadcast_to(table[0, pl.ds(t, 1), :], (16, 1024)), real),
            jnp.where(hit, jnp.broadcast_to(table[1, pl.ds(t, 1), :], (16, 1024)), imag),
        )

    zero = jnp.zeros((16, 1024), F32)
    chosen_parts = lax.fori_loop(0, 64, choose, (zero, zero))
    channel = (lax.broadcasted_iota(jnp.int32, (16, 1024), 1) // 2) % 4
    for po in range(2):
        for ci in range(4):
            weights[po * 64 + ci * 16 : po * 64 + ci * 16 + 16, :] = jnp.where(
                channel == ci, chosen_parts[po], 0.0
            ).astype(BF)

    def beam_power(c):
        first_frame, frames = BEAM_GROUPS[c]
        wait_all(*beam_args[c])
        fields = dot(weights[...], recv_beam[c].reshape(1024, LANES))
        power = fields[:64] * fields[:64] + fields[64:] * fields[64:]
        power_ref[:, first_frame : first_frame + frames] = power[:, :frames] + power[:, frames : 2 * frames]

    beam_power(0)
    beam_power(1)

    def hand_over(k):
        other = lax.rem(grp + k, GRP)
        return pltpu.make_async_remote_copy(
            src_ref=part_send.at[other],
            dst_ref=part_recv.at[k - 1],
            send_sem=part_send_sem.at[k - 1],
            recv_sem=part_recv_sem.at[k - 1],
            device_id=(stn, other),
            device_id_type=MESH,
        )

    load(2).wait()
    for c in range(3):
        if c == 2:
            pltpu.make_async_copy(
                send_spec.at[c, pl.ds(0, LATE - 1)], recv_spec.at[c, pl.ds(0, LATE - 1)], spec_send_sem.at[c]
            ).wait()
            send_all(*beam_args[2])
        wait_all(*spec_args[c])

        def gather_rows(b, _, c=c):
            block = recv_spec[c, pl.ds(b * 16, 16)].reshape(256, LANES)
            rows = dot(pick[...], block).astype(BF)
            wide = pl.ds(pl.multiple_of(b * 128, 128), 128)
            narrow = pl.ds(pl.multiple_of(b * 64, 64), 64)
            for e in range(2):
                at = 384 * e
                lanes = 2 * e * LANES
                lhs[wide, lanes : lanes + LANES] = rows[at : at + 128]
                lhs[wide, lanes + LANES : lanes + 2 * LANES] = rows[at + 128 : at + 256]
                rhs[narrow, lanes : lanes + LANES] = rows[at + 256 : at + 320]
                rhs[narrow, lanes + LANES : lanes + 2 * LANES] = rows[at + 320 : at + 384]
            return 0

        lax.fori_loop(0, 4, gather_rows, 0)
        for k in (1, 2, 3, 0):
            owner = lax.rem(grp + k, GRP)
            partial = dot_t(lhs[pl.ds(pl.multiple_of(owner * 128, 128), 128), :], rhs[...])
            if c > 0:
                partial = partial + part_own[k]
            if c < 2 or k == 0:
                part_own[k] = partial
            else:
                part_send[owner] = partial.astype(BF)
                hand_over(k).start()

    beam_power(2)

    total = part_own[0]
    for k in range(1, GRP):
        hand_over(k).wait_recv()
        total = total + part_recv[k - 1].astype(F32)
    vis_ref[...] = total * (1.0 / math.sqrt(4 * FRAMES * RADIX))

    for k in range(1, GRP):
        hand_over(k).wait_send()
    for c in range(3):
        wait_sent(*beam_args[c])
    for c in range(2):
        wait_sent(*spec_args[c])
    pltpu.make_async_copy(
        send_spec.at[2, pl.ds(0, STN - LATE)], recv_spec.at[2, pl.ds(0, STN - LATE)], late_sem
    ).wait()

    @pl.when(grp < GRP - 1)
    def _():
        for c in range(3):
            halo(c).wait_send()


def on_device(voltages, corr_taps, beam_taps, angle_table, table_index):
    x = voltages.reshape(8, TILES, LANES).transpose(1, 0, 2).reshape(HALF, 16, LANES)
    tables = [jnp.asarray(t) for t in constant_tables()]
    vmem = pl.BlockSpec(memory_space=pltpu.VMEM)
    dma = pltpu.SemaphoreType.DMA
    vis, power = pl.pallas_call(
        kernel,
        out_shape=(
            jax.ShapeDtypeStruct((128, 256), F32),
            jax.ShapeDtypeStruct((64, SHORT_FRAMES), F32),
        ),
        in_specs=[vmem] * 7 + [pl.BlockSpec(memory_space=pltpu.HBM)] * 3,
        out_specs=(vmem, vmem),
        scratch_shapes=[
            pltpu.VMEM((512, 512), BF),
            pltpu.VMEM((512, 512), BF),
            pltpu.VMEM((768, 256), BF),
            pltpu.VMEM((HALF, 16, LANES), BF),
            pltpu.VMEM((2 * TILES, 8, LANES), F32),
            pltpu.VMEM((2, SHORT_FRAMES * 8, LANES), F32),
            pltpu.VMEM((FRAMES * 256, LANES), F32),
            pltpu.VMEM((LANES, 512), BF),
            pltpu.VMEM((12 * RADIX, 512), BF),
            pltpu.VMEM((3, STN, 16, LANES), BF),
            pltpu.VMEM((3, STN, 16, LANES), BF),
            pltpu.VMEM((3, STN, 16, LANES), BF),
            pltpu.VMEM((3, STN, 16, LANES), BF),
            pltpu.VMEM((2, 64, 1024), F32),
            pltpu.VMEM((128, 1024), BF),
            pltpu.VMEM((512, 512), BF),
            pltpu.VMEM((256, 512), BF),
            pltpu.VMEM((GRP, 128, 256), F32),
            pltpu.VMEM((GRP, 128, 256), BF),
            pltpu.VMEM((GRP - 1, 128, 256), BF),
            pltpu.SemaphoreType.REGULAR,
            pltpu.SemaphoreType.REGULAR,
            dma((3,)),
            dma((3,)),
            dma((3,)),
            dma((3,)),
            dma((3,)),
            dma((3,)),
            dma((3,)),
            dma,
            dma((GRP - 1,)),
            dma((GRP - 1,)),
        ],
        compiler_params=pltpu.CompilerParams(
            collective_id=0, has_side_effects=True, vmem_limit_bytes=48 * 1024 * 1024
        ),
    )(x, corr_taps, beam_taps, angle_table, table_index, *tables)
    return vis.reshape(1, 64, 2, 256), power.reshape(4, 16, SHORT_FRAMES)


def solution(mesh):
    in_specs = (P(None, "stn", None, "grp"), P(), P(), P(), P())
    out_specs = (P("stn", "grp", None, None), P("stn", None, "grp"))
    return jax.shard_map(
        on_device, mesh=mesh, in_specs=in_specs, out_specs=out_specs, check_vma=False
    )
```

```python
import functools
import math

import jax
import jax.numpy as jnp
import ml_dtypes
import numpy as np
from jax import lax
from jax.experimental import pallas as pl
from jax.experimental.pallas import tpu as pltpu
from jax.sharding import PartitionSpec as P

MESH = pl.DeviceIdType.MESH
BF = jnp.bfloat16
F32 = jnp.float32

RADIX = 64
TAPS = 12
STN = 64
GRP = 4
LANES = 128
TILES = 352
HALF = 176
FRAMES = 11
SHORT_FRAMES = 176
LATE = 40
GROUPS = ((8, 3), (4, 4), (0, 4))
BEAM_GROUPS = ((112, 64), (48, 64), (0, 48))


def dft_tables(length):
    k = np.arange(length)
    phases = (k[:, None] * k[None, :] % length) * (2.0 * math.pi / length)
    factor = 1.0 / math.sqrt(length)
    return np.cos(phases) * factor, np.sin(phases) * factor


def constant_tables():
    bf = ml_dtypes.bfloat16
    cos, sin = dft_tables(RADIX)
    order = np.concatenate([np.arange(0, RADIX, 2), np.arange(1, RADIX, 2)])
    c, s = cos[order].T, sin[order].T
    first = np.block([[c, s], [-s, c]])
    k = np.arange(RADIX)
    phases = (k[:, None] * k[None, :]) * (2.0 * math.pi / (RADIX * RADIX))
    twist = np.stack([np.tile(np.cos(phases), (1, 4)), np.tile(np.sin(phases), (1, 4))])
    second = np.zeros((RADIX, 4, 2, 2, 4, RADIX))
    for q in range(4):
        second[:, q, 0, 0, q] = cos.T
        second[:, q, 0, 1, q] = sin.T
        second[:, q, 1, 0, q] = -sin.T
        second[:, q, 1, 1, q] = cos.T
    second = second.reshape(512, 512)
    cos, sin = dft_tables(256)
    short = np.zeros((256, 2, 2, 256))
    short[:, 0, 0] = cos.T
    short[:, 0, 1] = sin.T
    short[:, 1, 0] = -sin.T
    short[:, 1, 1] = cos.T
    short = short.reshape(512, 512)
    pick = np.zeros((2, 384, 16, 2, 4, 2))
    for pair in range(2):
        for src in range(16):
            for q in range(4):
                u = src * 4 + q
                pick[pair, 2 * u, src, pair, q, 0] = 1
                pick[pair, 2 * u + 1, src, pair, q, 1] = 1
                pick[pair, 128 + 2 * u, src, pair, q, 1] = 1
                pick[pair, 128 + 2 * u + 1, src, pair, q, 0] = -1
                pick[pair, 256 + u, src, pair, q, 0] = 1
                pick[pair, 320 + u, src, pair, q, 1] = 1
    pick_half = pick[0, :, :, 0].reshape(384, 128)
    pick = pick.reshape(768, 256)
    return (
        first.astype(bf),
        twist.astype(np.float32),
        second.astype(bf),
        short.astype(bf),
        pick.astype(bf),
        pick_half.astype(bf),
    )


def dot(a, b):
    return lax.dot_general(a, b, (((1,), (0,)), ((), ())), preferred_element_type=F32)


def dot_t(a, b):
    return lax.dot_general(a, b, (((1,), (1,)), ((), ())), preferred_element_type=F32)


def partner(stn, offset):
    y = lax.rem(stn // 32 + offset // 32, 2)
    z = lax.rem(lax.rem(stn // 4, 8) + lax.rem(offset // 4, 8), 8)
    x = lax.rem(lax.rem(stn, 4) + lax.rem(offset, 4), 4)
    return y * 32 + z * 4 + x


def kernel(
    x_ref, corr_taps, beam_taps, angles, index, first, twist, second_hbm, short_hbm, pick_hbm, pick_half_hbm,
    vis_ref, power_ref,
    second, short, pick, pick_half,
    hist, ext, fs, fl, z_ref, tw, tail_tw, send_beam, recv_beam, send_spec, recv_spec, send_half, recv_half,
    table, weights, lhs, rhs, part_own, part_send, part_recv,
    row_sem, column_sem, table_sem, halo_send, halo_recv,
    beam_send_sem, beam_recv_sem, spec_send_sem, spec_recv_sem, half_send_sem, half_recv_sem, late_sem,
    part_send_sem, part_recv_sem,
):
    stn = lax.axis_index("stn")
    grp = lax.axis_index("grp")

    barrier = pltpu.get_barrier_semaphore()
    lines = (1, 2, 3, 4, 8, 12, 16, 20, 24, 28, 32)
    for k in range(1, GRP):
        pl.semaphore_signal(
            barrier, inc=1, device_id=(stn, lax.rem(grp + k, GRP)), device_id_type=MESH
        )
    for k in lines:
        pl.semaphore_signal(
            barrier, inc=1, device_id=(partner(stn, k), grp), device_id_type=MESH
        )

    def load(i):
        source, target = ((short_hbm, short), (second_hbm, second), (pick_hbm, pick), (pick_half_hbm, pick_half))[i]
        return pltpu.make_async_copy(source, target, table_sem.at[i])

    for i in range(4):
        load(i).start()

    def widen_own(i, _):
        v = x_ref[i].astype(F32)
        ext[TILES + 2 * i] = v[:8]
        ext[TILES + 2 * i + 1] = v[8:]
        return 0

    lax.fori_loop(0, HALF, widen_own, 0, unroll=8)

    step = 8

    def short_filter(i, _):
        for a in range(2):
            taps = [
                jnp.broadcast_to(beam_taps[pl.ds(k, 1), a * LANES : (a + 1) * LANES], (8, LANES))
                for k in range(TAPS)
            ]
            base = TILES + i * (2 * step) + a
            window = [ext[base + 2 * j] for j in range(1 - TAPS, step)]
            for f in range(step):
                total = window[f + TAPS - 1] * taps[0]
                for k in range(1, TAPS):
                    total = total + window[f + TAPS - 1 - k] * taps[k]
                fs[a, pl.ds(pl.multiple_of((i * step + f) * 8, 8), 8), :] = total
        return 0

    def short_spectra(c, beside=None):
        first_frame, frames = BEAM_GROUPS[c]
        lax.fori_loop(first_frame // step, (first_frame + frames) // step, short_filter, 0)
        halves = []
        for st in range(2):
            for p in range(2):
                for part in range(2):
                    for a in range(2):
                        z_ref[pl.ds(p * frames, frames), pl.ds(part * 256 + a * LANES, LANES)] = fs[
                            a, pl.ds(first_frame * 8 + part * 4 + st * 2 + p, frames, stride=8), :
                        ].astype(BF)
            if frames < 64:
                z_ref[pl.ds(2 * frames, LANES - 2 * frames), :] = jnp.zeros((LANES - 2 * frames, 512), BF)
            halves.append(dot_t(short[...], z_ref[...]).reshape(STN, 8, LANES))
        block = jnp.concatenate(halves, axis=1)
        if beside is not None:
            block = block + beside
        send_beam[c] = block.astype(BF)

    load(0).wait()
    short_spectra(0)

    @pl.when(grp == 0)
    def _():
        def clear(i, _):
            ext[i] = jnp.zeros((8, LANES), F32)
            return 0

        lax.fori_loop(0, TILES, clear, 0, unroll=8)

    pl.semaphore_wait(barrier, len(lines) + GRP - 1)

    for k in (1, 2, 3):
        pl.semaphore_signal(row_sem, inc=1, device_id=(partner(stn, k), grp), device_id_type=MESH)

    def halo(c):
        first_frame, frames = GROUPS[c]
        at = pl.ds(16 * first_frame, 16 * frames)
        return pltpu.make_async_remote_copy(
            src_ref=x_ref.at[at],
            dst_ref=hist.at[at],
            send_sem=halo_send.at[c],
            recv_sem=halo_recv.at[c],
            device_id=(stn, lax.rem(grp + 1, GRP)),
            device_id_type=MESH,
        )

    def exchange(source, target, send_sem, recv_sem, k):
        other = partner(stn, k)
        return pltpu.make_async_remote_copy(
            src_ref=source.at[other],
            dst_ref=target.at[stn],
            send_sem=send_sem,
            recv_sem=recv_sem,
            device_id=(other, grp),
            device_id_type=MESH,
        )

    def send_all(source, target, send_sem, recv_sem, start=1, stop=STN):
        def body(k, _):
            exchange(source, target, send_sem, recv_sem, k).start()
            return 0

        lax.fori_loop(start, stop, body, 0)
        if start == 1:
            target[stn] = source[stn]

    def wait_all(source, target, send_sem, recv_sem):
        span = pl.ds(0, STN - 1)
        pltpu.make_async_copy(source.at[span], target.at[span], recv_sem).wait()

    def wait_sent(source, target, send_sem, recv_sem):
        span = pl.ds(0, STN - 1)
        pltpu.make_async_copy(source.at[span], target.at[span], send_sem).wait()

    beam_args = [
        (send_beam.at[c], recv_beam.at[c], beam_send_sem.at[c], beam_recv_sem.at[c]) for c in range(3)
    ]
    spec_args = [
        (send_spec.at[c], recv_spec.at[c], spec_send_sem.at[c], spec_recv_sem.at[c]) for c in range(2)
    ]
    half_args = (send_half, recv_half, half_send_sem, half_recv_sem)

    for k in range(4, STN // 2, 4):
        exchange(*beam_args[0], k).start()
    recv_beam[0, stn] = send_beam[0, stn]

    @pl.when(grp < GRP - 1)
    def _():
        for c in range(3):
            halo(c).start()

    pl.semaphore_wait(row_sem, 3)
    pl.semaphore_signal(column_sem, inc=1, device_id=(partner(stn, 32), grp), device_id_type=MESH)

    def to_plane(k, _):
        exchange(*beam_args[0], k + 1 + k // 3).start()
        return 0

    lax.fori_loop(0, 24, to_plane, 0)
    short_spectra(1)
    send_all(*beam_args[1], 1, STN // 2)

    pl.semaphore_wait(column_sem, 1)
    send_all(*beam_args[0], STN // 2, STN)

    low = lax.broadcasted_iota(jnp.int32, (32, LANES), 1) < RADIX
    tail_tw[...] = jnp.zeros((2 * LANES, 512), BF)

    for c, (first_frame, frames) in enumerate(GROUPS):

        @pl.when(grp > 0)
        def _(c=c, first_frame=first_frame, frames=frames):
            halo(c).wait_recv()

            def body(i, _):
                v = hist[i].astype(F32)
                ext[2 * i] = v[:8]
                ext[2 * i + 1] = v[8:]
                return 0

            lax.fori_loop(16 * first_frame, 16 * (first_frame + frames), body, 0, unroll=8)

        def long_filter(i, _, first_frame=first_frame, frames=frames):
            taps = [
                jnp.broadcast_to(
                    corr_taps[pl.ds(k, 1), pl.ds(pl.multiple_of(i * LANES, LANES), LANES)], (8, LANES)
                )
                for k in range(TAPS)
            ]
            window = [ext[i + 32 * (first_frame + m)] for m in range(frames + TAPS - 1)]
            for g in range(frames):
                total = window[g + TAPS - 1] * taps[0]
                for k in range(1, TAPS):
                    total = total + window[g + TAPS - 1 - k] * taps[k]
                fl[pl.ds(pl.multiple_of(((first_frame + g) * 32 + i) * 8, 8), 8), :] = total
            return 0

        lax.fori_loop(0, 32, long_filter, 0)

        def first_factor(g, _):
            rows = []
            for part in range(2):
                even, odd = [], []
                for q2 in range(2):
                    a = fl[pl.ds(g * 256 + part * 4 + 2 * q2, 32, stride=8), :]
                    b = fl[pl.ds(g * 256 + part * 4 + 2 * q2 + 1, 32, stride=8), :]
                    even.append(jnp.where(low, a, pltpu.roll(b, RADIX, 1)))
                    odd.append(jnp.where(low, pltpu.roll(a, RADIX, 1), b))
                rows.append(jnp.concatenate(even, axis=1))
                rows.append(jnp.concatenate(odd, axis=1))
            out = dot(first[...], jnp.concatenate(rows, axis=0).astype(BF))
            real, imag = out[:RADIX], out[RADIX:]
            at = pl.ds(pl.multiple_of(g * RADIX, RADIX), RADIX)
            tw[at, 0:256] = (real * twist[0] + imag * twist[1]).astype(BF)
            tw[at, 256:512] = (imag * twist[0] - real * twist[1]).astype(BF)
            return 0

        lax.fori_loop(first_frame, first_frame + frames, first_factor, 0)

        def second_factor(rows):
            return dot_t(second[...], rows).reshape(STN, 8, LANES)

        if c == 0:
            load(1).wait()
            send_half[...] = second_factor(tw[8 * RADIX : 10 * RADIX, :]).astype(BF)
            send_all(*half_args)
            tail_tw[96:128, :] = tw[640:672, :]
            tail_tw[224:256, :] = tw[672:704, :]
            tail = [second_factor(tail_tw[e * LANES : (e + 1) * LANES, :]) for e in range(2)]
            short_spectra(2, jnp.concatenate(tail, axis=1))
            send_all(*beam_args[2])
        else:
            pairs = [
                second_factor(tw[at : at + LANES, :])
                for at in (first_frame * RADIX, first_frame * RADIX + LANES)
            ]
            send_spec[c - 1] = jnp.concatenate(pairs, axis=1).astype(BF)
            if c == 1:
                send_all(*spec_args[0])
            else:
                send_all(*spec_args[1], 1, LATE)
                send_all(send_spec.at[1], recv_spec.at[1], late_sem, spec_recv_sem.at[1], LATE, STN)

    shape = (256, 1024)
    column = lax.broadcasted_iota(jnp.int32, shape, 1)
    match = lax.broadcasted_iota(jnp.int32, shape, 0) == stn * 4 + (column // 2) % 4
    own_re = jnp.where(match & (column % 2 == 0), 1.0, 0.0).astype(BF)
    own_im = jnp.where(match & (column % 2 == 1), 1.0, 0.0).astype(BF)
    factor = 1.0 / math.sqrt(2 * STN)
    cos = (jnp.cos(angles[...]) * factor).astype(BF)
    sin = (jnp.sin(angles[...]) * factor).astype(BF)
    table[0] = dot(cos, own_re) - dot(sin, own_im)
    table[1] = dot(sin, own_re) + dot(cos, own_im)
    shape = (128, 1024)
    spread = jnp.where(
        lax.broadcasted_iota(jnp.int32, shape, 0) == lax.broadcasted_iota(jnp.int32, shape, 1) // 8,
        1.0,
        0.0,
    ).astype(BF)
    chosen = dot(index[...].astype(F32).astype(BF), spread)

    def choose(t, carry):
        real, imag = carry
        hit = chosen == t.astype(F32)
        return (
            jnp.where(hit, jnp.broadcast_to(table[0, pl.ds(t, 1), :], (16, 1024)), real),
            jnp.where(hit, jnp.broadcast_to(table[1, pl.ds(t, 1), :], (16, 1024)), imag),
        )

    zero = jnp.zeros((16, 1024), F32)
    chosen_parts = lax.fori_loop(0, 64, choose, (zero, zero))
    channel = (lax.broadcasted_iota(jnp.int32, (16, 1024), 1) // 2) % 4
    for po in range(2):
        for ci in range(4):
            weights[po * 64 + ci * 16 : po * 64 + ci * 16 + 16, :] = jnp.where(
                channel == ci, chosen_parts[po], 0.0
            ).astype(BF)

    def beam_power(c):
        first_frame, frames = BEAM_GROUPS[c]
        wait_all(*beam_args[c])
        fields = dot(weights[...], recv_beam[c].reshape(1024, LANES))
        power = fields[:64] * fields[:64] + fields[64:] * fields[64:]
        power_ref[:, first_frame : first_frame + frames] = power[:, :frames] + power[:, frames : 2 * frames]

    beam_power(0)

    def hand_over(k):
        other = lax.rem(grp + k, GRP)
        return pltpu.make_async_remote_copy(
            src_ref=part_send.at[other],
            dst_ref=part_recv.at[k - 1],
            send_sem=part_send_sem.at[k - 1],
            recv_sem=part_recv_sem.at[k - 1],
            device_id=(stn, other),
            device_id_type=MESH,
        )

    def correlate(source, selection, pairs, masked, first_block, last_block):
        rows_each = source.shape[1]

        def gather_rows(b, _):
            block = source[pl.ds(b * 16, 16)].reshape(16 * rows_each, LANES)
            rows = dot(selection[...], block)
            if masked:
                rows = jnp.where(lax.broadcasted_iota(jnp.int32, rows.shape, 1) >= 96, rows, 0.0)
            rows = rows.astype(BF)
            wide = pl.ds(pl.multiple_of(b * 128, 128), 128)
            narrow = pl.ds(pl.multiple_of(b * 64, 64), 64)
            for e in range(pairs):
                at = 384 * e
                lanes = 2 * e * LANES
                lhs[wide, lanes : lanes + LANES] = rows[at : at + 128]
                lhs[wide, lanes + LANES : lanes + 2 * LANES] = rows[at + 128 : at + 256]
                rhs[narrow, lanes : lanes + LANES] = rows[at + 256 : at + 320]
                rhs[narrow, lanes + LANES : lanes + 2 * LANES] = rows[at + 320 : at + 384]
            return 0

        lax.fori_loop(0, 4, gather_rows, 0)
        depth = 2 * pairs * LANES
        for k in (1, 2, 3, 0):
            owner = lax.rem(grp + k, GRP)
            partial = dot_t(lhs[pl.ds(pl.multiple_of(owner * 128, 128), 128), 0:depth], rhs[:, 0:depth])
            if not first_block:
                partial = partial + part_own[k]
            if not last_block or k == 0:
                part_own[k] = partial
            else:
                part_send[owner] = partial.astype(BF)
                hand_over(k).start()

    load(2).wait()
    load(3).wait()
    wait_all(*half_args)
    correlate(recv_half, pick_half, 1, False, True, False)
    beam_power(2)
    correlate(recv_beam.at[2], pick, 2, True, False, False)
    wait_all(*spec_args[0])
    correlate(recv_spec.at[0], pick, 2, False, False, False)
    pltpu.make_async_copy(
        send_spec.at[1, pl.ds(0, LATE - 1)], recv_spec.at[1, pl.ds(0, LATE - 1)], spec_send_sem.at[1]
    ).wait()
    send_all(*beam_args[1], STN // 2, STN)
    wait_all(*spec_args[1])
    correlate(recv_spec.at[1], pick, 2, False, False, True)

    beam_power(1)

    total = part_own[0]
    for k in range(1, GRP):
        hand_over(k).wait_recv()
        total = total + part_recv[k - 1].astype(F32)
    vis_ref[...] = total * (1.0 / math.sqrt(4 * FRAMES * RADIX))

    for k in range(1, GRP):
        hand_over(k).wait_send()
    for c in range(3):
        wait_sent(*beam_args[c])
    wait_sent(*half_args)
    wait_sent(*spec_args[0])
    pltpu.make_async_copy(
        send_spec.at[1, pl.ds(0, STN - LATE)], recv_spec.at[1, pl.ds(0, STN - LATE)], late_sem
    ).wait()

    @pl.when(grp < GRP - 1)
    def _():
        for c in range(3):
            halo(c).wait_send()


def on_device(voltages, corr_taps, beam_taps, angle_table, table_index):
    x = voltages.reshape(8, TILES, LANES).transpose(1, 0, 2).reshape(HALF, 16, LANES)
    tables = [jnp.asarray(t) for t in constant_tables()]
    vmem = pl.BlockSpec(memory_space=pltpu.VMEM)
    dma = pltpu.SemaphoreType.DMA
    vis, power = pl.pallas_call(
        kernel,
        out_shape=(
            jax.ShapeDtypeStruct((128, 256), F32),
            jax.ShapeDtypeStruct((64, SHORT_FRAMES), F32),
        ),
        in_specs=[vmem] * 7 + [pl.BlockSpec(memory_space=pltpu.HBM)] * 4,
        out_specs=(vmem, vmem),
        scratch_shapes=[
            pltpu.VMEM((512, 512), BF),
            pltpu.VMEM((512, 512), BF),
            pltpu.VMEM((768, 256), BF),
            pltpu.VMEM((384, LANES), BF),
            pltpu.VMEM((HALF, 16, LANES), BF),
            pltpu.VMEM((2 * TILES, 8, LANES), F32),
            pltpu.VMEM((2, SHORT_FRAMES * 8, LANES), F32),
            pltpu.VMEM((FRAMES * 256, LANES), F32),
            pltpu.VMEM((LANES, 512), BF),
            pltpu.VMEM((FRAMES * RADIX, 512), BF),
            pltpu.VMEM((2 * LANES, 512), BF),
            pltpu.VMEM((3, STN, 16, LANES), BF),
            pltpu.VMEM((3, STN, 16, LANES), BF),
            pltpu.VMEM((2, STN, 16, LANES), BF),
            pltpu.VMEM((2, STN, 16, LANES), BF),
            pltpu.VMEM((STN, 8, LANES), BF),
            pltpu.VMEM((STN, 8, LANES), BF),
            pltpu.VMEM((2, 64, 1024), F32),
            pltpu.VMEM((128, 1024), BF),
            pltpu.VMEM((512, 512), BF),
            pltpu.VMEM((256, 512), BF),
            pltpu.VMEM((GRP, 128, 256), F32),
            pltpu.VMEM((GRP, 128, 256), BF),
            pltpu.VMEM((GRP - 1, 128, 256), BF),
            pltpu.SemaphoreType.REGULAR,
            pltpu.SemaphoreType.REGULAR,
            dma((4,)),
            dma((3,)),
            dma((3,)),
            dma((3,)),
            dma((3,)),
            dma((2,)),
            dma((2,)),
            dma,
            dma,
            dma,
            dma((GRP - 1,)),
            dma((GRP - 1,)),
        ],
        compiler_params=pltpu.CompilerParams(
            collective_id=0, has_side_effects=True, vmem_limit_bytes=48 * 1024 * 1024
        ),
    )(x, corr_taps, beam_taps, angle_table, table_index, *tables)
    return vis.reshape(1, 64, 2, 256), power.reshape(4, 16, SHORT_FRAMES)


def solution(mesh):
    in_specs = (P(None, "stn", None, "grp"), P(), P(), P(), P())
    out_specs = (P("stn", "grp", None, None), P("stn", None, "grp"))
    return jax.shard_map(
        on_device, mesh=mesh, in_specs=in_specs, out_specs=out_specs, check_vma=False
    )
```

```python
import functools
import math

import jax
import jax.numpy as jnp
import ml_dtypes
import numpy as np
from jax import lax
from jax.experimental import pallas as pl
from jax.experimental.pallas import tpu as pltpu
from jax.sharding import PartitionSpec as P

MESH = pl.DeviceIdType.MESH
BF = jnp.bfloat16
F32 = jnp.float32

RADIX = 64
TAPS = 12
STN = 64
GRP = 4
LANES = 128
TILES = 352
HALF = 176
FRAMES = 11
SHORT_FRAMES = 176
LATE = 16
GROUPS = ((8, 3), (4, 4), (0, 4))
BEAM_GROUPS = ((112, 64), (48, 64), (0, 48))


def dft_tables(length):
    k = np.arange(length)
    phases = (k[:, None] * k[None, :] % length) * (2.0 * math.pi / length)
    factor = 1.0 / math.sqrt(length)
    return np.cos(phases) * factor, np.sin(phases) * factor


def constant_tables():
    bf = ml_dtypes.bfloat16
    cos, sin = dft_tables(RADIX)
    order = np.concatenate([np.arange(0, RADIX, 2), np.arange(1, RADIX, 2)])
    c, s = cos[order].T, sin[order].T
    first = np.block([[c, s], [-s, c]])
    k = np.arange(RADIX)
    phases = (k[:, None] * k[None, :]) * (2.0 * math.pi / (RADIX * RADIX))
    twist = np.stack([np.tile(np.cos(phases), (1, 4)), np.tile(np.sin(phases), (1, 4))])
    second = np.zeros((RADIX, 4, 2, 2, 4, RADIX))
    for q in range(4):
        second[:, q, 0, 0, q] = cos.T
        second[:, q, 0, 1, q] = sin.T
        second[:, q, 1, 0, q] = -sin.T
        second[:, q, 1, 1, q] = cos.T
    second = second.reshape(512, 512)
    cos, sin = dft_tables(256)
    short = np.zeros((256, 2, 2, 256))
    short[:, 0, 0] = cos.T
    short[:, 0, 1] = sin.T
    short[:, 1, 0] = -sin.T
    short[:, 1, 1] = cos.T
    short = short.reshape(512, 512)
    pick = np.zeros((2, 384, 16, 2, 4, 2))
    for pair in range(2):
        for src in range(16):
            for q in range(4):
                u = src * 4 + q
                pick[pair, 2 * u, src, pair, q, 0] = 1
                pick[pair, 2 * u + 1, src, pair, q, 1] = 1
                pick[pair, 128 + 2 * u, src, pair, q, 1] = 1
                pick[pair, 128 + 2 * u + 1, src, pair, q, 0] = -1
                pick[pair, 256 + u, src, pair, q, 0] = 1
                pick[pair, 320 + u, src, pair, q, 1] = 1
    pick_half = pick[0, :, :, 0].reshape(384, 128)
    pick = pick.reshape(768, 256)
    return (
        first.astype(bf),
        twist.astype(np.float32),
        second.astype(bf),
        short.astype(bf),
        pick.astype(bf),
        pick_half.astype(bf),
    )


def dot(a, b):
    return lax.dot_general(a, b, (((1,), (0,)), ((), ())), preferred_element_type=F32)


def dot_t(a, b):
    return lax.dot_general(a, b, (((1,), (1,)), ((), ())), preferred_element_type=F32)


def partner(stn, offset):
    y = lax.rem(stn // 32 + offset // 32, 2)
    z = lax.rem(lax.rem(stn // 4, 8) + lax.rem(offset // 4, 8), 8)
    x = lax.rem(lax.rem(stn, 4) + lax.rem(offset, 4), 4)
    return y * 32 + z * 4 + x


def kernel(
    volts_hbm, corr_taps_hbm, beam_taps_hbm, angles_hbm, index_hbm, first_hbm, twist_hbm, second_hbm,
    short_hbm, pick_hbm, pick_half_hbm,
    vis_ref, power_ref,
    second, short, pick, pick_half, volts, corr_taps, beam_taps, angles, index, first, twist,
    x_ref, hist, ext, fs, fl, z_ref, tw, tail_tw, send_beam, recv_beam, send_spec, recv_spec, send_half, recv_half,
    table, weights, lhs, rhs, part_own, part_send, part_recv,
    row_sem, column_sem, table_sem, halo_send, halo_recv,
    beam_send_sem, beam_recv_sem, spec_send_sem, spec_recv_sem, half_send_sem, half_recv_sem, late_sem,
    part_send_sem, part_recv_sem,
):
    stn = lax.axis_index("stn")
    grp = lax.axis_index("grp")

    barrier = pltpu.get_barrier_semaphore()
    lines = (1, 2, 3, 4, 8, 12, 16, 20, 24, 28, 32)
    for k in range(1, GRP):
        pl.semaphore_signal(
            barrier, inc=1, device_id=(stn, lax.rem(grp + k, GRP)), device_id_type=MESH
        )
    for k in lines:
        pl.semaphore_signal(
            barrier, inc=1, device_id=(partner(stn, k), grp), device_id_type=MESH
        )

    def load(i):
        source, target = (
            (volts_hbm, volts),
            (beam_taps_hbm, beam_taps),
            (short_hbm, short),
            (corr_taps_hbm, corr_taps),
            (first_hbm, first),
            (twist_hbm, twist),
            (second_hbm, second),
            (angles_hbm, angles),
            (index_hbm, index),
            (pick_hbm, pick),
            (pick_half_hbm, pick_half),
        )[i]
        return pltpu.make_async_copy(source, target, table_sem.at[i])

    for i in range(11):
        load(i).start()

    def widen_own(i, _):
        both = []
        for e in range(2):
            at = pl.ds(pl.multiple_of((2 * i + e) * LANES, LANES), LANES)
            v = jnp.concatenate([volts[j, :, at].astype(F32) for j in range(4)], axis=0)
            ext[TILES + 2 * i + e] = v
            both.append(v)
        x_ref[i] = jnp.concatenate(both, axis=0).astype(BF)
        return 0

    load(0).wait()
    lax.fori_loop(0, HALF, widen_own, 0, unroll=8)

    step = 8

    def short_filter(i, _):
        for a in range(2):
            taps = [
                jnp.broadcast_to(beam_taps[pl.ds(k, 1), a * LANES : (a + 1) * LANES], (8, LANES))
                for k in range(TAPS)
            ]
            base = TILES + i * (2 * step) + a
            window = [ext[base + 2 * j] for j in range(1 - TAPS, step)]
            for f in range(step):
                total = window[f + TAPS - 1] * taps[0]
                for k in range(1, TAPS):
                    total = total + window[f + TAPS - 1 - k] * taps[k]
                fs[a, pl.ds(pl.multiple_of((i * step + f) * 8, 8), 8), :] = total
        return 0

    def short_spectra(c, beside=None):
        first_frame, frames = BEAM_GROUPS[c]
        lax.fori_loop(first_frame // step, (first_frame + frames) // step, short_filter, 0)
        halves = []
        for st in range(2):
            for p in range(2):
                for part in range(2):
                    for a in range(2):
                        z_ref[pl.ds(p * frames, frames), pl.ds(part * 256 + a * LANES, LANES)] = fs[
                            a, pl.ds(first_frame * 8 + part * 4 + st * 2 + p, frames, stride=8), :
                        ].astype(BF)
            if frames < 64:
                z_ref[pl.ds(2 * frames, LANES - 2 * frames), :] = jnp.zeros((LANES - 2 * frames, 512), BF)
            halves.append(dot_t(short[...], z_ref[...]).reshape(STN, 8, LANES))
        block = jnp.concatenate(halves, axis=1)
        if beside is not None:
            block = block + beside
        send_beam[c] = block.astype(BF)

    load(1).wait()
    load(2).wait()
    short_spectra(0)

    @pl.when(grp == 0)
    def _():
        def clear(i, _):
            ext[i] = jnp.zeros((8, LANES), F32)
            return 0

        lax.fori_loop(0, TILES, clear, 0, unroll=8)

    pl.semaphore_wait(barrier, len(lines) + GRP - 1)

    for k in (1, 2, 3):
        pl.semaphore_signal(row_sem, inc=1, device_id=(partner(stn, k), grp), device_id_type=MESH)

    def halo(c):
        first_frame, frames = GROUPS[c]
        at = pl.ds(16 * first_frame, 16 * frames)
        return pltpu.make_async_remote_copy(
            src_ref=x_ref.at[at],
            dst_ref=hist.at[at],
            send_sem=halo_send.at[c],
            recv_sem=halo_recv.at[c],
            device_id=(stn, lax.rem(grp + 1, GRP)),
            device_id_type=MESH,
        )

    def exchange(source, target, send_sem, recv_sem, k):
        other = partner(stn, k)
        return pltpu.make_async_remote_copy(
            src_ref=source.at[other],
            dst_ref=target.at[stn],
            send_sem=send_sem,
            recv_sem=recv_sem,
            device_id=(other, grp),
            device_id_type=MESH,
        )

    def send_all(source, target, send_sem, recv_sem, start=1, stop=STN):
        def body(k, _):
            exchange(source, target, send_sem, recv_sem, k).start()
            return 0

        lax.fori_loop(start, stop, body, 0)
        if start == 1:
            target[stn] = source[stn]

    def wait_all(source, target, send_sem, recv_sem):
        span = pl.ds(0, STN - 1)
        pltpu.make_async_copy(source.at[span], target.at[span], recv_sem).wait()

    def wait_sent(source, target, send_sem, recv_sem):
        span = pl.ds(0, STN - 1)
        pltpu.make_async_copy(source.at[span], target.at[span], send_sem).wait()

    beam_args = [
        (send_beam.at[c], recv_beam.at[c], beam_send_sem.at[c], beam_recv_sem.at[c]) for c in range(3)
    ]
    spec_args = [
        (send_spec.at[c], recv_spec.at[c], spec_send_sem.at[c], spec_recv_sem.at[c]) for c in range(2)
    ]
    half_args = (send_half, recv_half, half_send_sem, half_recv_sem)

    for k in range(4, STN // 2, 4):
        exchange(*beam_args[0], k).start()
    recv_beam[0, stn] = send_beam[0, stn]

    @pl.when(grp < GRP - 1)
    def _():
        for c in range(3):
            halo(c).start()

    pl.semaphore_wait(row_sem, 3)
    pl.semaphore_signal(column_sem, inc=1, device_id=(partner(stn, 32), grp), device_id_type=MESH)

    def to_plane(k, _):
        exchange(*beam_args[0], k + 1 + k // 3).start()
        return 0

    lax.fori_loop(0, 24, to_plane, 0)
    short_spectra(1)
    send_all(*beam_args[1], 1, STN // 2)

    pl.semaphore_wait(column_sem, 1)
    send_all(*beam_args[0], STN // 2, STN)

    for i in range(3, 11):
        load(i).wait()
    low = lax.broadcasted_iota(jnp.int32, (32, LANES), 1) < RADIX
    tail_tw[...] = jnp.zeros((2 * LANES, 512), BF)

    for c, (first_frame, frames) in enumerate(GROUPS):

        @pl.when(grp > 0)
        def _(c=c, first_frame=first_frame, frames=frames):
            halo(c).wait_recv()

            def body(i, _):
                v = hist[i].astype(F32)
                ext[2 * i] = v[:8]
                ext[2 * i + 1] = v[8:]
                return 0

            lax.fori_loop(16 * first_frame, 16 * (first_frame + frames), body, 0, unroll=8)

        def long_filter(i, _, first_frame=first_frame, frames=frames):
            taps = [
                jnp.broadcast_to(
                    corr_taps[pl.ds(k, 1), pl.ds(pl.multiple_of(i * LANES, LANES), LANES)], (8, LANES)
                )
                for k in range(TAPS)
            ]
            window = [ext[i + 32 * (first_frame + m)] for m in range(frames + TAPS - 1)]
            for g in range(frames):
                total = window[g + TAPS - 1] * taps[0]
                for k in range(1, TAPS):
                    total = total + window[g + TAPS - 1 - k] * taps[k]
                fl[pl.ds(pl.multiple_of(((first_frame + g) * 32 + i) * 8, 8), 8), :] = total
            return 0

        lax.fori_loop(0, 32, long_filter, 0)

        def first_factor(g, _):
            rows = []
            for part in range(2):
                even, odd = [], []
                for q2 in range(2):
                    a = fl[pl.ds(g * 256 + part * 4 + 2 * q2, 32, stride=8), :]
                    b = fl[pl.ds(g * 256 + part * 4 + 2 * q2 + 1, 32, stride=8), :]
                    even.append(jnp.where(low, a, pltpu.roll(b, RADIX, 1)))
                    odd.append(jnp.where(low, pltpu.roll(a, RADIX, 1), b))
                rows.append(jnp.concatenate(even, axis=1))
                rows.append(jnp.concatenate(odd, axis=1))
            out = dot(first[...], jnp.concatenate(rows, axis=0).astype(BF))
            real, imag = out[:RADIX], out[RADIX:]
            at = pl.ds(pl.multiple_of(g * RADIX, RADIX), RADIX)
            tw[at, 0:256] = (real * twist[0] + imag * twist[1]).astype(BF)
            tw[at, 256:512] = (imag * twist[0] - real * twist[1]).astype(BF)
            return 0

        lax.fori_loop(first_frame, first_frame + frames, first_factor, 0)

        def second_factor(rows):
            return dot_t(second[...], rows).reshape(STN, 8, LANES)

        if c == 0:
            send_half[...] = second_factor(tw[8 * RADIX : 10 * RADIX, :]).astype(BF)
            send_all(*half_args)
            tail_tw[96:128, :] = tw[640:672, :]
            tail_tw[224:256, :] = tw[672:704, :]
            tail = [second_factor(tail_tw[e * LANES : (e + 1) * LANES, :]) for e in range(2)]
            short_spectra(2, jnp.concatenate(tail, axis=1))
            send_all(*beam_args[2])
        else:
            pairs = [
                second_factor(tw[at : at + LANES, :])
                for at in (first_frame * RADIX, first_frame * RADIX + LANES)
            ]
            send_spec[c - 1] = jnp.concatenate(pairs, axis=1).astype(BF)
            if c == 1:
                send_all(*spec_args[0])
            else:
                send_all(*spec_args[1], 1, LATE)
                send_all(send_spec.at[1], recv_spec.at[1], late_sem, spec_recv_sem.at[1], LATE, STN)

    shape = (256, 1024)
    column = lax.broadcasted_iota(jnp.int32, shape, 1)
    match = lax.broadcasted_iota(jnp.int32, shape, 0) == stn * 4 + (column // 2) % 4
    own_re = jnp.where(match & (column % 2 == 0), 1.0, 0.0).astype(BF)
    own_im = jnp.where(match & (column % 2 == 1), 1.0, 0.0).astype(BF)
    factor = 1.0 / math.sqrt(2 * STN)
    cos = (jnp.cos(angles[...]) * factor).astype(BF)
    sin = (jnp.sin(angles[...]) * factor).astype(BF)
    table[0] = dot(cos, own_re) - dot(sin, own_im)
    table[1] = dot(sin, own_re) + dot(cos, own_im)
    shape = (128, 1024)
    spread = jnp.where(
        lax.broadcasted_iota(jnp.int32, shape, 0) == lax.broadcasted_iota(jnp.int32, shape, 1) // 8,
        1.0,
        0.0,
    ).astype(BF)
    chosen = dot(index[...].astype(F32).astype(BF), spread)

    def choose(t, carry):
        real, imag = carry
        hit = chosen == t.astype(F32)
        return (
            jnp.where(hit, jnp.broadcast_to(table[0, pl.ds(t, 1), :], (16, 1024)), real),
            jnp.where(hit, jnp.broadcast_to(table[1, pl.ds(t, 1), :], (16, 1024)), imag),
        )

    zero = jnp.zeros((16, 1024), F32)
    chosen_parts = lax.fori_loop(0, 64, choose, (zero, zero))
    channel = (lax.broadcasted_iota(jnp.int32, (16, 1024), 1) // 2) % 4
    for po in range(2):
        for ci in range(4):
            weights[po * 64 + ci * 16 : po * 64 + ci * 16 + 16, :] = jnp.where(
                channel == ci, chosen_parts[po], 0.0
            ).astype(BF)

    def beam_power(c):
        first_frame, frames = BEAM_GROUPS[c]
        wait_all(*beam_args[c])
        fields = dot(weights[...], recv_beam[c].reshape(1024, LANES))
        power = fields[:64] * fields[:64] + fields[64:] * fields[64:]
        power_ref[:, first_frame : first_frame + frames] = power[:, :frames] + power[:, frames : 2 * frames]

    beam_power(0)

    def hand_over(k):
        other = lax.rem(grp + k, GRP)
        return pltpu.make_async_remote_copy(
            src_ref=part_send.at[other],
            dst_ref=part_recv.at[k - 1],
            send_sem=part_send_sem.at[k - 1],
            recv_sem=part_recv_sem.at[k - 1],
            device_id=(stn, other),
            device_id_type=MESH,
        )

    def correlate(source, selection, pairs, masked, first_block, last_block):
        rows_each = source.shape[1]

        def gather_rows(b, _):
            block = source[pl.ds(b * 16, 16)].reshape(16 * rows_each, LANES)
            rows = dot(selection[...], block)
            if masked:
                rows = jnp.where(lax.broadcasted_iota(jnp.int32, rows.shape, 1) >= 96, rows, 0.0)
            rows = rows.astype(BF)
            wide = pl.ds(pl.multiple_of(b * 128, 128), 128)
            narrow = pl.ds(pl.multiple_of(b * 64, 64), 64)
            for e in range(pairs):
                at = 384 * e
                lanes = 2 * e * LANES
                lhs[wide, lanes : lanes + LANES] = rows[at : at + 128]
                lhs[wide, lanes + LANES : lanes + 2 * LANES] = rows[at + 128 : at + 256]
                rhs[narrow, lanes : lanes + LANES] = rows[at + 256 : at + 320]
                rhs[narrow, lanes + LANES : lanes + 2 * LANES] = rows[at + 320 : at + 384]
            return 0

        lax.fori_loop(0, 4, gather_rows, 0)
        depth = 2 * pairs * LANES
        for k in (1, 2, 3, 0):
            owner = lax.rem(grp + k, GRP)
            partial = dot_t(lhs[pl.ds(pl.multiple_of(owner * 128, 128), 128), 0:depth], rhs[:, 0:depth])
            if not first_block:
                partial = partial + part_own[k]
            if not last_block or k == 0:
                part_own[k] = partial
            else:
                part_send[owner] = partial.astype(BF)
                hand_over(k).start()

    wait_all(*half_args)
    correlate(recv_half, pick_half, 1, False, True, False)
    beam_power(2)
    correlate(recv_beam.at[2], pick, 2, True, False, False)
    wait_all(*spec_args[0])
    correlate(recv_spec.at[0], pick, 2, False, False, False)
    pltpu.make_async_copy(
        send_spec.at[1, pl.ds(0, LATE - 1)], recv_spec.at[1, pl.ds(0, LATE - 1)], spec_send_sem.at[1]
    ).wait()
    send_all(*beam_args[1], STN // 2, STN)
    wait_all(*spec_args[1])
    correlate(recv_spec.at[1], pick, 2, False, False, True)

    beam_power(1)

    total = part_own[0]
    for k in range(1, GRP):
        hand_over(k).wait_recv()
        total = total + part_recv[k - 1].astype(F32)
    total = total * (1.0 / math.sqrt(4 * FRAMES * RADIX))
    for u in range(64):
        vis_ref[0, u] = total[2 * u : 2 * u + 2]

    for k in range(1, GRP):
        hand_over(k).wait_send()
    for c in range(3):
        wait_sent(*beam_args[c])
    wait_sent(*half_args)
    wait_sent(*spec_args[0])
    pltpu.make_async_copy(
        send_spec.at[1, pl.ds(0, STN - LATE)], recv_spec.at[1, pl.ds(0, STN - LATE)], late_sem
    ).wait()

    @pl.when(grp < GRP - 1)
    def _():
        for c in range(3):
            halo(c).wait_send()


def on_device(voltages, corr_taps, beam_taps, angle_table, table_index):
    volts = voltages.reshape(4, 2, TILES * LANES)
    tables = [jnp.asarray(t) for t in constant_tables()]
    vmem = pl.BlockSpec(memory_space=pltpu.VMEM)
    dma = pltpu.SemaphoreType.DMA
    vis, power = pl.pallas_call(
        kernel,
        out_shape=(
            jax.ShapeDtypeStruct((1, 64, 2, 256), F32),
            jax.ShapeDtypeStruct((64, SHORT_FRAMES), F32),
        ),
        in_specs=[pl.BlockSpec(memory_space=pl.ANY)] * 11,
        out_specs=(vmem, vmem),
        scratch_shapes=[
            pltpu.VMEM((512, 512), BF),
            pltpu.VMEM((512, 512), BF),
            pltpu.VMEM((768, 256), BF),
            pltpu.VMEM((384, LANES), BF),
            pltpu.VMEM((4, 2, TILES * LANES), BF),
            pltpu.VMEM((TAPS, RADIX * RADIX), F32),
            pltpu.VMEM((TAPS, 256), F32),
            pltpu.VMEM((64, 256), F32),
            pltpu.VMEM((16, 128), jnp.int32),
            pltpu.VMEM((128, 128), BF),
            pltpu.VMEM((2, 64, 256), F32),
            pltpu.VMEM((HALF, 16, LANES), BF),
            pltpu.VMEM((HALF, 16, LANES), BF),
            pltpu.VMEM((2 * TILES, 8, LANES), F32),
            pltpu.VMEM((2, SHORT_FRAMES * 8, LANES), F32),
            pltpu.VMEM((FRAMES * 256, LANES), F32),
            pltpu.VMEM((LANES, 512), BF),
            pltpu.VMEM((FRAMES * RADIX, 512), BF),
            pltpu.VMEM((2 * LANES, 512), BF),
            pltpu.VMEM((3, STN, 16, LANES), BF),
            pltpu.VMEM((3, STN, 16, LANES), BF),
            pltpu.VMEM((2, STN, 16, LANES), BF),
            pltpu.VMEM((2, STN, 16, LANES), BF),
            pltpu.VMEM((STN, 8, LANES), BF),
            pltpu.VMEM((STN, 8, LANES), BF),
            pltpu.VMEM((2, 64, 1024), F32),
            pltpu.VMEM((128, 1024), BF),
            pltpu.VMEM((512, 512), BF),
            pltpu.VMEM((256, 512), BF),
            pltpu.VMEM((GRP, 128, 256), F32),
            pltpu.VMEM((GRP, 128, 256), BF),
            pltpu.VMEM((GRP - 1, 128, 256), BF),
            pltpu.SemaphoreType.REGULAR,
            pltpu.SemaphoreType.REGULAR,
            dma((11,)),
            dma((3,)),
            dma((3,)),
            dma((3,)),
            dma((3,)),
            dma((2,)),
            dma((2,)),
            dma,
            dma,
            dma,
            dma((GRP - 1,)),
            dma((GRP - 1,)),
        ],
        compiler_params=pltpu.CompilerParams(
            collective_id=0, has_side_effects=True, vmem_limit_bytes=60 * 1024 * 1024
        ),
    )(volts, corr_taps, beam_taps, angle_table, table_index, *tables)
    return vis, power.reshape(4, 16, SHORT_FRAMES)


def solution(mesh):
    in_specs = (P(None, "stn", None, "grp"), P(), P(), P(), P())
    out_specs = (P("stn", "grp", None, None), P("stn", None, "grp"))
    return jax.shard_map(
        on_device, mesh=mesh, in_specs=in_specs, out_specs=out_specs, check_vma=False
    )
```

```python
import functools
import math

import jax
import jax.numpy as jnp
import ml_dtypes
import numpy as np
from jax import lax
from jax.experimental import pallas as pl
from jax.experimental.pallas import tpu as pltpu
from jax.sharding import PartitionSpec as P

MESH = pl.DeviceIdType.MESH
BF = jnp.bfloat16
F32 = jnp.float32

RADIX = 64
TAPS = 12
STN = 64
GRP = 4
LANES = 128
TILES = 352
HALF = 176
FRAMES = 11
SHORT_FRAMES = 176
LATE = 16
GROUPS = ((8, 3), (4, 4), (0, 4))
BEAM_GROUPS = ((112, 64), (48, 64), (0, 48))


def dft_tables(length):
    k = np.arange(length)
    phases = (k[:, None] * k[None, :] % length) * (2.0 * math.pi / length)
    factor = 1.0 / math.sqrt(length)
    return np.cos(phases) * factor, np.sin(phases) * factor


def constant_tables():
    bf = ml_dtypes.bfloat16
    cos, sin = dft_tables(RADIX)
    order = np.concatenate([np.arange(0, RADIX, 2), np.arange(1, RADIX, 2)])
    c, s = cos[order].T, sin[order].T
    first = np.block([[c, s], [-s, c]])
    k = np.arange(RADIX)
    phases = (k[:, None] * k[None, :]) * (2.0 * math.pi / (RADIX * RADIX))
    twist = np.stack([np.tile(np.cos(phases), (1, 4)), np.tile(np.sin(phases), (1, 4))])
    second = np.zeros((RADIX, 4, 2, 2, 4, RADIX))
    for q in range(4):
        second[:, q, 0, 0, q] = cos.T
        second[:, q, 0, 1, q] = sin.T
        second[:, q, 1, 0, q] = -sin.T
        second[:, q, 1, 1, q] = cos.T
    second = second.reshape(512, 512)
    cos, sin = dft_tables(256)
    short = np.zeros((256, 2, 2, 256))
    short[:, 0, 0] = cos.T
    short[:, 0, 1] = sin.T
    short[:, 1, 0] = -sin.T
    short[:, 1, 1] = cos.T
    short = short.reshape(512, 512)
    pick = np.zeros((2, 384, 16, 2, 4, 2))
    for pair in range(2):
        for src in range(16):
            for q in range(4):
                u = src * 4 + q
                pick[pair, 2 * u, src, pair, q, 0] = 1
                pick[pair, 2 * u + 1, src, pair, q, 1] = 1
                pick[pair, 128 + 2 * u, src, pair, q, 1] = 1
                pick[pair, 128 + 2 * u + 1, src, pair, q, 0] = -1
                pick[pair, 256 + u, src, pair, q, 0] = 1
                pick[pair, 320 + u, src, pair, q, 1] = 1
    pick_half = pick[0, :, :, 0].reshape(384, 128)
    pick = pick.reshape(768, 256)
    return (
        first.astype(bf),
        twist.astype(np.float32),
        second.astype(bf),
        short.astype(bf),
        pick.astype(bf),
        pick_half.astype(bf),
    )


def dot(a, b):
    return lax.dot_general(a, b, (((1,), (0,)), ((), ())), preferred_element_type=F32)


def dot_t(a, b):
    return lax.dot_general(a, b, (((1,), (1,)), ((), ())), preferred_element_type=F32)


def partner(stn, offset):
    y = lax.rem(stn // 32 + offset // 32, 2)
    z = lax.rem(lax.rem(stn // 4, 8) + lax.rem(offset // 4, 8), 8)
    x = lax.rem(lax.rem(stn, 4) + lax.rem(offset, 4), 4)
    return y * 32 + z * 4 + x


def kernel(
    volts_hbm, corr_taps_hbm, beam_taps_hbm, angles_hbm, index_hbm, first_hbm, twist_hbm, second_hbm,
    short_hbm, pick_hbm, pick_half_hbm,
    vis_ref, power_ref,
    second, short, pick, pick_half, volts, corr_taps, beam_taps, angles, index, first, twist,
    x_ref, hist, ext, fs, fl, z_ref, tw, tail_tw, send_beam, recv_beam, send_spec, recv_spec, send_half, recv_half,
    table, weights, lhs, rhs, part_own, part_send, part_recv,
    row_sem, column_sem, table_sem, halo_send, halo_recv,
    beam_send_sem, beam_recv_sem, spec_send_sem, spec_recv_sem, half_send_sem, half_recv_sem, late_sem,
    part_send_sem, part_recv_sem,
):
    stn = lax.axis_index("stn")
    grp = lax.axis_index("grp")

    barrier = pltpu.get_barrier_semaphore()
    lines = (1, 2, 3, 4, 8, 12, 16, 20, 24, 28, 32)
    for k in range(1, GRP):
        pl.semaphore_signal(
            barrier, inc=1, device_id=(stn, lax.rem(grp + k, GRP)), device_id_type=MESH
        )
    for k in lines:
        pl.semaphore_signal(
            barrier, inc=1, device_id=(partner(stn, k), grp), device_id_type=MESH
        )

    def load(i):
        source, target = (
            (volts_hbm, volts),
            (beam_taps_hbm, beam_taps),
            (short_hbm, short),
            (corr_taps_hbm, corr_taps),
            (first_hbm, first),
            (twist_hbm, twist),
            (second_hbm, second),
            (angles_hbm, angles),
            (index_hbm, index),
            (pick_hbm, pick),
            (pick_half_hbm, pick_half),
        )[i]
        return pltpu.make_async_copy(source, target, table_sem.at[i])

    for i in range(11):
        load(i).start()

    def widen_own(i, _):
        both = []
        for e in range(2):
            at = pl.ds(pl.multiple_of((2 * i + e) * LANES, LANES), LANES)
            v = jnp.concatenate([volts[j, :, at].astype(F32) for j in range(4)], axis=0)
            ext[TILES + 2 * i + e] = v
            both.append(v)
        x_ref[i] = jnp.concatenate(both, axis=0).astype(BF)
        return 0

    load(0).wait()
    lax.fori_loop(96, HALF, widen_own, 0, unroll=8)

    step = 8

    def short_filter(i, _):
        for a in range(2):
            taps = [
                jnp.broadcast_to(beam_taps[pl.ds(k, 1), a * LANES : (a + 1) * LANES], (8, LANES))
                for k in range(TAPS)
            ]
            base = TILES + i * (2 * step) + a
            window = [ext[base + 2 * j] for j in range(1 - TAPS, step)]
            for f in range(step):
                total = window[f + TAPS - 1] * taps[0]
                for k in range(1, TAPS):
                    total = total + window[f + TAPS - 1 - k] * taps[k]
                fs[a, pl.ds(pl.multiple_of((i * step + f) * 8, 8), 8), :] = total
        return 0

    def short_spectra(c, beside=None):
        first_frame, frames = BEAM_GROUPS[c]
        lax.fori_loop(first_frame // step, (first_frame + frames) // step, short_filter, 0)
        halves = []
        for st in range(2):
            for p in range(2):
                for part in range(2):
                    for a in range(2):
                        z_ref[pl.ds(p * frames, frames), pl.ds(part * 256 + a * LANES, LANES)] = fs[
                            a, pl.ds(first_frame * 8 + part * 4 + st * 2 + p, frames, stride=8), :
                        ].astype(BF)
            if frames < 64:
                z_ref[pl.ds(2 * frames, LANES - 2 * frames), :] = jnp.zeros((LANES - 2 * frames, 512), BF)
            halves.append(dot_t(short[...], z_ref[...]).reshape(STN, 8, LANES))
        block = jnp.concatenate(halves, axis=1)
        if beside is not None:
            block = block + beside
        send_beam[c] = block.astype(BF)

    load(1).wait()
    load(2).wait()
    short_spectra(0)

    @pl.when(grp == 0)
    def _():
        def clear(i, _):
            ext[i] = jnp.zeros((8, LANES), F32)
            return 0

        lax.fori_loop(0, TILES, clear, 0, unroll=8)

    pl.semaphore_wait(barrier, len(lines) + GRP - 1)

    for k in (1, 2, 3):
        pl.semaphore_signal(row_sem, inc=1, device_id=(partner(stn, k), grp), device_id_type=MESH)

    def halo(c):
        first_frame, frames = GROUPS[c]
        at = pl.ds(16 * first_frame, 16 * frames)
        return pltpu.make_async_remote_copy(
            src_ref=x_ref.at[at],
            dst_ref=hist.at[at],
            send_sem=halo_send.at[c],
            recv_sem=halo_recv.at[c],
            device_id=(stn, lax.rem(grp + 1, GRP)),
            device_id_type=MESH,
        )

    def exchange(source, target, send_sem, recv_sem, k):
        other = partner(stn, k)
        return pltpu.make_async_remote_copy(
            src_ref=source.at[other],
            dst_ref=target.at[stn],
            send_sem=send_sem,
            recv_sem=recv_sem,
            device_id=(other, grp),
            device_id_type=MESH,
        )

    def send_all(source, target, send_sem, recv_sem, start=1, stop=STN):
        def body(k, _):
            exchange(source, target, send_sem, recv_sem, k).start()
            return 0

        lax.fori_loop(start, stop, body, 0)
        if start == 1:
            target[stn] = source[stn]

    def wait_all(source, target, send_sem, recv_sem):
        span = pl.ds(0, STN - 1)
        pltpu.make_async_copy(source.at[span], target.at[span], recv_sem).wait()

    def wait_sent(source, target, send_sem, recv_sem):
        span = pl.ds(0, STN - 1)
        pltpu.make_async_copy(source.at[span], target.at[span], send_sem).wait()

    beam_args = [
        (send_beam.at[c], recv_beam.at[c], beam_send_sem.at[c], beam_recv_sem.at[c]) for c in range(3)
    ]
    spec_args = [
        (send_spec.at[c], recv_spec.at[c], spec_send_sem.at[c], spec_recv_sem.at[c]) for c in range(2)
    ]
    half_args = (send_half, recv_half, half_send_sem, half_recv_sem)

    for k in range(4, STN // 2, 4):
        exchange(*beam_args[0], k).start()
    recv_beam[0, stn] = send_beam[0, stn]

    @pl.when(grp < GRP - 1)
    def _():
        halo(0).start()

    pl.semaphore_wait(row_sem, 3)
    pl.semaphore_signal(column_sem, inc=1, device_id=(partner(stn, 32), grp), device_id_type=MESH)

    def to_plane(k, _):
        exchange(*beam_args[0], k + 1 + k // 3).start()
        return 0

    lax.fori_loop(0, 24, to_plane, 0)
    lax.fori_loop(0, 96, widen_own, 0, unroll=8)

    @pl.when(grp < GRP - 1)
    def _():
        halo(1).start()
        halo(2).start()

    short_spectra(1)
    send_all(*beam_args[1], 1, STN // 2)

    pl.semaphore_wait(column_sem, 1)
    send_all(*beam_args[0], STN // 2, STN)

    for i in range(3, 11):
        load(i).wait()
    low = lax.broadcasted_iota(jnp.int32, (32, LANES), 1) < RADIX
    tail_tw[...] = jnp.zeros((2 * LANES, 512), BF)

    for c, (first_frame, frames) in enumerate(GROUPS):

        @pl.when(grp > 0)
        def _(c=c, first_frame=first_frame, frames=frames):
            halo(c).wait_recv()

            def body(i, _):
                v = hist[i].astype(F32)
                ext[2 * i] = v[:8]
                ext[2 * i + 1] = v[8:]
                return 0

            lax.fori_loop(16 * first_frame, 16 * (first_frame + frames), body, 0, unroll=8)

        def long_filter(i, _, first_frame=first_frame, frames=frames):
            taps = [
                jnp.broadcast_to(
                    corr_taps[pl.ds(k, 1), pl.ds(pl.multiple_of(i * LANES, LANES), LANES)], (8, LANES)
                )
                for k in range(TAPS)
            ]
            window = [ext[i + 32 * (first_frame + m)] for m in range(frames + TAPS - 1)]
            for g in range(frames):
                total = window[g + TAPS - 1] * taps[0]
                for k in range(1, TAPS):
                    total = total + window[g + TAPS - 1 - k] * taps[k]
                fl[pl.ds(pl.multiple_of(((first_frame + g) * 32 + i) * 8, 8), 8), :] = total
            return 0

        lax.fori_loop(0, 32, long_filter, 0)

        def first_factor(g, _):
            rows = []
            for part in range(2):
                even, odd = [], []
                for q2 in range(2):
                    a = fl[pl.ds(g * 256 + part * 4 + 2 * q2, 32, stride=8), :]
                    b = fl[pl.ds(g * 256 + part * 4 + 2 * q2 + 1, 32, stride=8), :]
                    even.append(jnp.where(low, a, pltpu.roll(b, RADIX, 1)))
                    odd.append(jnp.where(low, pltpu.roll(a, RADIX, 1), b))
                rows.append(jnp.concatenate(even, axis=1))
                rows.append(jnp.concatenate(odd, axis=1))
            out = dot(first[...], jnp.concatenate(rows, axis=0).astype(BF))
            real, imag = out[:RADIX], out[RADIX:]
            at = pl.ds(pl.multiple_of(g * RADIX, RADIX), RADIX)
            tw[at, 0:256] = (real * twist[0] + imag * twist[1]).astype(BF)
            tw[at, 256:512] = (imag * twist[0] - real * twist[1]).astype(BF)
            return 0

        lax.fori_loop(first_frame, first_frame + frames, first_factor, 0)

        def second_factor(rows):
            return dot_t(second[...], rows).reshape(STN, 8, LANES)

        if c == 0:
            send_half[...] = second_factor(tw[8 * RADIX : 10 * RADIX, :]).astype(BF)
            send_all(*half_args)
            tail_tw[96:128, :] = tw[640:672, :]
            tail_tw[224:256, :] = tw[672:704, :]
            tail = [second_factor(tail_tw[e * LANES : (e + 1) * LANES, :]) for e in range(2)]
            short_spectra(2, jnp.concatenate(tail, axis=1))
            send_all(*beam_args[2])
        else:
            pairs = [
                second_factor(tw[at : at + LANES, :])
                for at in (first_frame * RADIX, first_frame * RADIX + LANES)
            ]
            send_spec[c - 1] = jnp.concatenate(pairs, axis=1).astype(BF)
            if c == 1:
                send_all(*spec_args[0])
            else:
                send_all(*spec_args[1], 1, LATE)
                send_all(send_spec.at[1], recv_spec.at[1], late_sem, spec_recv_sem.at[1], LATE, STN)

    shape = (256, 1024)
    column = lax.broadcasted_iota(jnp.int32, shape, 1)
    match = lax.broadcasted_iota(jnp.int32, shape, 0) == stn * 4 + (column // 2) % 4
    own_re = jnp.where(match & (column % 2 == 0), 1.0, 0.0).astype(BF)
    own_im = jnp.where(match & (column % 2 == 1), 1.0, 0.0).astype(BF)
    factor = 1.0 / math.sqrt(2 * STN)
    cos = (jnp.cos(angles[...]) * factor).astype(BF)
    sin = (jnp.sin(angles[...]) * factor).astype(BF)
    table[0] = dot(cos, own_re) - dot(sin, own_im)
    table[1] = dot(sin, own_re) + dot(cos, own_im)
    shape = (128, 1024)
    spread = jnp.where(
        lax.broadcasted_iota(jnp.int32, shape, 0) == lax.broadcasted_iota(jnp.int32, shape, 1) // 8,
        1.0,
        0.0,
    ).astype(BF)
    chosen = dot(index[...].astype(F32).astype(BF), spread)

    def choose(t, carry):
        real, imag = carry
        hit = chosen == t.astype(F32)
        return (
            jnp.where(hit, jnp.broadcast_to(table[0, pl.ds(t, 1), :], (16, 1024)), real),
            jnp.where(hit, jnp.broadcast_to(table[1, pl.ds(t, 1), :], (16, 1024)), imag),
        )

    zero = jnp.zeros((16, 1024), F32)
    chosen_parts = lax.fori_loop(0, 64, choose, (zero, zero))
    channel = (lax.broadcasted_iota(jnp.int32, (16, 1024), 1) // 2) % 4
    for po in range(2):
        for ci in range(4):
            weights[po * 64 + ci * 16 : po * 64 + ci * 16 + 16, :] = jnp.where(
                channel == ci, chosen_parts[po], 0.0
            ).astype(BF)

    def beam_power(c):
        first_frame, frames = BEAM_GROUPS[c]
        wait_all(*beam_args[c])
        fields = dot(weights[...], recv_beam[c].reshape(1024, LANES))
        power = fields[:64] * fields[:64] + fields[64:] * fields[64:]
        power_ref[:, first_frame : first_frame + frames] = power[:, :frames] + power[:, frames : 2 * frames]

    beam_power(0)

    def hand_over(k):
        other = lax.rem(grp + k, GRP)
        return pltpu.make_async_remote_copy(
            src_ref=part_send.at[other],
            dst_ref=part_recv.at[k - 1],
            send_sem=part_send_sem.at[k - 1],
            recv_sem=part_recv_sem.at[k - 1],
            device_id=(stn, other),
            device_id_type=MESH,
        )

    def correlate(source, selection, pairs, masked, first_block, last_block):
        rows_each = source.shape[1]

        def gather_rows(b, _):
            block = source[pl.ds(b * 16, 16)].reshape(16 * rows_each, LANES)
            rows = dot(selection[...], block)
            if masked:
                rows = jnp.where(lax.broadcasted_iota(jnp.int32, rows.shape, 1) >= 96, rows, 0.0)
            rows = rows.astype(BF)
            wide = pl.ds(pl.multiple_of(b * 128, 128), 128)
            narrow = pl.ds(pl.multiple_of(b * 64, 64), 64)
            for e in range(pairs):
                at = 384 * e
                lanes = 2 * e * LANES
                lhs[wide, lanes : lanes + LANES] = rows[at : at + 128]
                lhs[wide, lanes + LANES : lanes + 2 * LANES] = rows[at + 128 : at + 256]
                rhs[narrow, lanes : lanes + LANES] = rows[at + 256 : at + 320]
                rhs[narrow, lanes + LANES : lanes + 2 * LANES] = rows[at + 320 : at + 384]
            return 0

        lax.fori_loop(0, 4, gather_rows, 0)
        depth = 2 * pairs * LANES
        for k in (1, 2, 3, 0):
            owner = lax.rem(grp + k, GRP)
            partial = dot_t(lhs[pl.ds(pl.multiple_of(owner * 128, 128), 128), 0:depth], rhs[:, 0:depth])
            if not first_block:
                partial = partial + part_own[k]
            if not last_block or k == 0:
                part_own[k] = partial
            else:
                part_send[owner] = partial.astype(BF)
                hand_over(k).start()

    wait_all(*half_args)
    correlate(recv_half, pick_half, 1, False, True, False)
    beam_power(2)
    correlate(recv_beam.at[2], pick, 2, True, False, False)
    wait_all(*spec_args[0])
    correlate(recv_spec.at[0], pick, 2, False, False, False)
    pltpu.make_async_copy(
        send_spec.at[1, pl.ds(0, LATE - 1)], recv_spec.at[1, pl.ds(0, LATE - 1)], spec_send_sem.at[1]
    ).wait()
    send_all(*beam_args[1], STN // 2, STN)
    wait_all(*spec_args[1])
    correlate(recv_spec.at[1], pick, 2, False, False, True)

    beam_power(1)

    total = part_own[0]
    for k in range(1, GRP):
        hand_over(k).wait_recv()
        total = total + part_recv[k - 1].astype(F32)
    total = total * (1.0 / math.sqrt(4 * FRAMES * RADIX))
    for u in range(64):
        vis_ref[0, u] = total[2 * u : 2 * u + 2]

    for k in range(1, GRP):
        hand_over(k).wait_send()
    for c in range(3):
        wait_sent(*beam_args[c])
    wait_sent(*half_args)
    wait_sent(*spec_args[0])
    pltpu.make_async_copy(
        send_spec.at[1, pl.ds(0, STN - LATE)], recv_spec.at[1, pl.ds(0, STN - LATE)], late_sem
    ).wait()

    @pl.when(grp < GRP - 1)
    def _():
        for c in range(3):
            halo(c).wait_send()


def on_device(voltages, corr_taps, beam_taps, angle_table, table_index):
    volts = voltages.reshape(4, 2, TILES * LANES)
    tables = [jnp.asarray(t) for t in constant_tables()]
    vmem = pl.BlockSpec(memory_space=pltpu.VMEM)
    dma = pltpu.SemaphoreType.DMA
    vis, power = pl.pallas_call(
        kernel,
        out_shape=(
            jax.ShapeDtypeStruct((1, 64, 2, 256), F32),
            jax.ShapeDtypeStruct((64, SHORT_FRAMES), F32),
        ),
        in_specs=[pl.BlockSpec(memory_space=pl.ANY)] * 11,
        out_specs=(vmem, vmem),
        scratch_shapes=[
            pltpu.VMEM((512, 512), BF),
            pltpu.VMEM((512, 512), BF),
            pltpu.VMEM((768, 256), BF),
            pltpu.VMEM((384, LANES), BF),
            pltpu.VMEM((4, 2, TILES * LANES), BF),
            pltpu.VMEM((TAPS, RADIX * RADIX), F32),
            pltpu.VMEM((TAPS, 256), F32),
            pltpu.VMEM((64, 256), F32),
            pltpu.VMEM((16, 128), jnp.int32),
            pltpu.VMEM((128, 128), BF),
            pltpu.VMEM((2, 64, 256), F32),
            pltpu.VMEM((HALF, 16, LANES), BF),
            pltpu.VMEM((HALF, 16, LANES), BF),
            pltpu.VMEM((2 * TILES, 8, LANES), F32),
            pltpu.VMEM((2, SHORT_FRAMES * 8, LANES), F32),
            pltpu.VMEM((FRAMES * 256, LANES), F32),
            pltpu.VMEM((LANES, 512), BF),
            pltpu.VMEM((FRAMES * RADIX, 512), BF),
            pltpu.VMEM((2 * LANES, 512), BF),
            pltpu.VMEM((3, STN, 16, LANES), BF),
            pltpu.VMEM((3, STN, 16, LANES), BF),
            pltpu.VMEM((2, STN, 16, LANES), BF),
            pltpu.VMEM((2, STN, 16, LANES), BF),
            pltpu.VMEM((STN, 8, LANES), BF),
            pltpu.VMEM((STN, 8, LANES), BF),
            pltpu.VMEM((2, 64, 1024), F32),
            pltpu.VMEM((128, 1024), BF),
            pltpu.VMEM((512, 512), BF),
            pltpu.VMEM((256, 512), BF),
            pltpu.VMEM((GRP, 128, 256), F32),
            pltpu.VMEM((GRP, 128, 256), BF),
            pltpu.VMEM((GRP - 1, 128, 256), BF),
            pltpu.SemaphoreType.REGULAR,
            pltpu.SemaphoreType.REGULAR,
            dma((11,)),
            dma((3,)),
            dma((3,)),
            dma((3,)),
            dma((3,)),
            dma((2,)),
            dma((2,)),
            dma,
            dma,
            dma,
            dma((GRP - 1,)),
            dma((GRP - 1,)),
        ],
        compiler_params=pltpu.CompilerParams(
            collective_id=0, has_side_effects=True, vmem_limit_bytes=60 * 1024 * 1024
        ),
    )(volts, corr_taps, beam_taps, angle_table, table_index, *tables)
    return vis, power.reshape(4, 16, SHORT_FRAMES)


def solution(mesh):
    in_specs = (P(None, "stn", None, "grp"), P(), P(), P(), P())
    out_specs = (P("stn", "grp", None, None), P("stn", None, "grp"))
    return jax.shard_map(
        on_device, mesh=mesh, in_specs=in_specs, out_specs=out_specs, check_vma=False
    )
```

```python
import functools
import math

import jax
import jax.numpy as jnp
import ml_dtypes
import numpy as np
from jax import lax
from jax.experimental import pallas as pl
from jax.experimental.pallas import tpu as pltpu
from jax.sharding import PartitionSpec as P

MESH = pl.DeviceIdType.MESH
BF = jnp.bfloat16
F32 = jnp.float32

RADIX = 64
TAPS = 12
STN = 64
GRP = 4
LANES = 128
TILES = 352
HALF = 176
FRAMES = 11
SHORT_FRAMES = 176
LATE = 16
GROUPS = ((8, 3), (4, 4), (0, 4))
BEAM_GROUPS = ((112, 64), (48, 64), (0, 48))


def dft_tables(length):
    k = np.arange(length)
    phases = (k[:, None] * k[None, :] % length) * (2.0 * math.pi / length)
    factor = 1.0 / math.sqrt(length)
    return np.cos(phases) * factor, np.sin(phases) * factor


def constant_tables():
    bf = ml_dtypes.bfloat16
    cos, sin = dft_tables(RADIX)
    order = np.concatenate([np.arange(0, RADIX, 2), np.arange(1, RADIX, 2)])
    c, s = cos[order].T, sin[order].T
    first = np.block([[c, s], [-s, c]])
    k = np.arange(RADIX)
    phases = (k[:, None] * k[None, :]) * (2.0 * math.pi / (RADIX * RADIX))
    twist = np.stack([np.tile(np.cos(phases), (1, 4)), np.tile(np.sin(phases), (1, 4))])
    second = np.zeros((RADIX, 4, 2, 2, 4, RADIX))
    for q in range(4):
        second[:, q, 0, 0, q] = cos.T
        second[:, q, 0, 1, q] = sin.T
        second[:, q, 1, 0, q] = -sin.T
        second[:, q, 1, 1, q] = cos.T
    second = second.reshape(512, 512)
    cos, sin = dft_tables(256)
    short = np.zeros((256, 2, 2, 256))
    short[:, 0, 0] = cos.T
    short[:, 0, 1] = sin.T
    short[:, 1, 0] = -sin.T
    short[:, 1, 1] = cos.T
    short = short.reshape(512, 512)
    pick = np.zeros((2, 384, 16, 2, 4, 2))
    for pair in range(2):
        for src in range(16):
            for q in range(4):
                u = src * 4 + q
                pick[pair, 2 * u, src, pair, q, 0] = 1
                pick[pair, 2 * u + 1, src, pair, q, 1] = 1
                pick[pair, 128 + 2 * u, src, pair, q, 1] = 1
                pick[pair, 128 + 2 * u + 1, src, pair, q, 0] = -1
                pick[pair, 256 + u, src, pair, q, 0] = 1
                pick[pair, 320 + u, src, pair, q, 1] = 1
    pick_half = pick[0, :, :, 0].reshape(384, 128)
    pick = pick.reshape(768, 256)
    return (
        first.astype(bf),
        twist.astype(np.float32),
        second.astype(bf),
        short.astype(bf),
        pick.astype(bf),
        pick_half.astype(bf),
    )


def dot(a, b):
    return lax.dot_general(a, b, (((1,), (0,)), ((), ())), preferred_element_type=F32)


def dot_t(a, b):
    return lax.dot_general(a, b, (((1,), (1,)), ((), ())), preferred_element_type=F32)


def partner(stn, offset):
    y = lax.rem(stn // 32 + offset // 32, 2)
    z = lax.rem(lax.rem(stn // 4, 8) + lax.rem(offset // 4, 8), 8)
    x = lax.rem(lax.rem(stn, 4) + lax.rem(offset, 4), 4)
    return y * 32 + z * 4 + x


def kernel(
    volts_hbm, corr_taps_hbm, beam_taps_hbm, angles_hbm, index_hbm, first_hbm, twist_hbm, second_hbm,
    short_hbm, pick_hbm, pick_half_hbm,
    vis_ref, power_ref,
    second, short, pick, pick_half, volts, corr_taps, beam_taps, angles, index, first, twist,
    x_ref, hist, ext, fs, fl, z_ref, tw, tail_tw, send_beam, recv_beam, send_spec, recv_spec, send_half, recv_half,
    table, weights, lhs, rhs, part_own, part_send, part_recv,
    row_sem, column_sem, table_sem, halo_send, halo_recv,
    beam_send_sem, beam_recv_sem, spec_send_sem, spec_recv_sem, half_send_sem, half_recv_sem, late_sem,
    part_send_sem, part_recv_sem,
):
    stn = lax.axis_index("stn")
    grp = lax.axis_index("grp")

    barrier = pltpu.get_barrier_semaphore()
    lines = (1, 2, 3, 4, 8, 12, 16, 20, 24, 28, 32)
    for k in range(1, GRP):
        pl.semaphore_signal(
            barrier, inc=1, device_id=(stn, lax.rem(grp + k, GRP)), device_id_type=MESH
        )
    for k in lines:
        pl.semaphore_signal(
            barrier, inc=1, device_id=(partner(stn, k), grp), device_id_type=MESH
        )

    def load(i):
        source, target = (
            (volts_hbm, volts),
            (beam_taps_hbm, beam_taps),
            (short_hbm, short),
            (corr_taps_hbm, corr_taps),
            (first_hbm, first),
            (twist_hbm, twist),
            (second_hbm, second),
            (angles_hbm, angles),
            (index_hbm, index),
            (pick_hbm, pick),
            (pick_half_hbm, pick_half),
        )[i]
        return pltpu.make_async_copy(source, target, table_sem.at[i])

    for i in range(11):
        load(i).start()

    def widen_own(i, _):
        both = []
        for e in range(2):
            at = pl.ds(pl.multiple_of((2 * i + e) * LANES, LANES), LANES)
            v = jnp.concatenate([volts[j, :, at].astype(F32) for j in range(4)], axis=0)
            ext[TILES + 2 * i + e] = v
            both.append(v)
        x_ref[i] = jnp.concatenate(both, axis=0).astype(BF)
        return 0

    load(0).wait()
    lax.fori_loop(96, HALF, widen_own, 0, unroll=8)

    step = 8

    def short_filter(i, _):
        for a in range(2):
            taps = [
                jnp.broadcast_to(beam_taps[pl.ds(k, 1), a * LANES : (a + 1) * LANES], (8, LANES))
                for k in range(TAPS)
            ]
            base = TILES + i * (2 * step) + a
            window = [ext[base + 2 * j] for j in range(1 - TAPS, step)]
            for f in range(step):
                total = window[f + TAPS - 1] * taps[0]
                for k in range(1, TAPS):
                    total = total + window[f + TAPS - 1 - k] * taps[k]
                fs[a, pl.ds(pl.multiple_of((i * step + f) * 8, 8), 8), :] = total
        return 0

    def short_spectra(c, beside=None):
        first_frame, frames = BEAM_GROUPS[c]
        lax.fori_loop(first_frame // step, (first_frame + frames) // step, short_filter, 0)
        halves = []
        for st in range(2):
            for p in range(2):
                for part in range(2):
                    for a in range(2):
                        z_ref[pl.ds(p * frames, frames), pl.ds(part * 256 + a * LANES, LANES)] = fs[
                            a, pl.ds(first_frame * 8 + part * 4 + st * 2 + p, frames, stride=8), :
                        ].astype(BF)
            if frames < 64:
                z_ref[pl.ds(2 * frames, LANES - 2 * frames), :] = jnp.zeros((LANES - 2 * frames, 512), BF)
            halves.append(dot_t(short[...], z_ref[...]).reshape(STN, 8, LANES))
        block = jnp.concatenate(halves, axis=1)
        if beside is not None:
            block = block + beside
        send_beam[c] = block.astype(BF)

    load(1).wait()
    load(2).wait()
    short_spectra(0)

    @pl.when(grp == 0)
    def _():
        def clear(i, _):
            ext[i] = jnp.zeros((8, LANES), F32)
            return 0

        lax.fori_loop(0, TILES, clear, 0, unroll=8)

    pl.semaphore_wait(barrier, len(lines) + GRP - 1)

    for k in (1, 2, 3):
        pl.semaphore_signal(row_sem, inc=1, device_id=(partner(stn, k), grp), device_id_type=MESH)

    def halo(c):
        first_frame, frames = GROUPS[c]
        at = pl.ds(16 * first_frame, 16 * frames)
        return pltpu.make_async_remote_copy(
            src_ref=x_ref.at[at],
            dst_ref=hist.at[at],
            send_sem=halo_send.at[c],
            recv_sem=halo_recv.at[c],
            device_id=(stn, lax.rem(grp + 1, GRP)),
            device_id_type=MESH,
        )

    def exchange(source, target, send_sem, recv_sem, k):
        other = partner(stn, k)
        return pltpu.make_async_remote_copy(
            src_ref=source.at[other],
            dst_ref=target.at[stn],
            send_sem=send_sem,
            recv_sem=recv_sem,
            device_id=(other, grp),
            device_id_type=MESH,
        )

    def send_all(source, target, send_sem, recv_sem, start=1, stop=STN):
        def body(k, _):
            exchange(source, target, send_sem, recv_sem, k).start()
            return 0

        lax.fori_loop(start, stop, body, 0)
        if start == 1:
            target[stn] = source[stn]

    def wait_all(source, target, send_sem, recv_sem):
        span = pl.ds(0, STN - 1)
        pltpu.make_async_copy(source.at[span], target.at[span], recv_sem).wait()

    def wait_sent(source, target, send_sem, recv_sem):
        span = pl.ds(0, STN - 1)
        pltpu.make_async_copy(source.at[span], target.at[span], send_sem).wait()

    beam_args = [
        (send_beam.at[c], recv_beam.at[c], beam_send_sem.at[c], beam_recv_sem.at[c]) for c in range(3)
    ]
    spec_args = [
        (send_spec.at[c], recv_spec.at[c], spec_send_sem.at[c], spec_recv_sem.at[c]) for c in range(2)
    ]
    half_args = (send_half, recv_half, half_send_sem, half_recv_sem)

    for k in range(4, STN // 2, 4):
        exchange(*beam_args[0], k).start()
    recv_beam[0, stn] = send_beam[0, stn]

    @pl.when(grp < GRP - 1)
    def _():
        halo(0).start()

    pl.semaphore_wait(row_sem, 3)
    pl.semaphore_signal(column_sem, inc=1, device_id=(partner(stn, 32), grp), device_id_type=MESH)

    def to_plane(k, _):
        exchange(*beam_args[0], k + 1 + k // 3).start()
        return 0

    lax.fori_loop(0, 24, to_plane, 0)
    lax.fori_loop(0, 96, widen_own, 0, unroll=8)

    @pl.when(grp < GRP - 1)
    def _():
        halo(1).start()
        halo(2).start()

    short_spectra(1)
    send_all(*beam_args[1], 1, STN // 2)

    pl.semaphore_wait(column_sem, 1)
    send_all(*beam_args[0], STN // 2, 48)

    for i in range(3, 11):
        load(i).wait()
    low = lax.broadcasted_iota(jnp.int32, (32, LANES), 1) < RADIX
    tail_tw[...] = jnp.zeros((2 * LANES, 512), BF)

    for c, (first_frame, frames) in enumerate(GROUPS):

        @pl.when(grp > 0)
        def _(c=c, first_frame=first_frame, frames=frames):
            halo(c).wait_recv()

            def body(i, _):
                v = hist[i].astype(F32)
                ext[2 * i] = v[:8]
                ext[2 * i + 1] = v[8:]
                return 0

            lax.fori_loop(16 * first_frame, 16 * (first_frame + frames), body, 0, unroll=8)

        def long_filter(i, _, first_frame=first_frame, frames=frames):
            taps = [
                jnp.broadcast_to(
                    corr_taps[pl.ds(k, 1), pl.ds(pl.multiple_of(i * LANES, LANES), LANES)], (8, LANES)
                )
                for k in range(TAPS)
            ]
            window = [ext[i + 32 * (first_frame + m)] for m in range(frames + TAPS - 1)]
            for g in range(frames):
                total = window[g + TAPS - 1] * taps[0]
                for k in range(1, TAPS):
                    total = total + window[g + TAPS - 1 - k] * taps[k]
                fl[pl.ds(pl.multiple_of(((first_frame + g) * 32 + i) * 8, 8), 8), :] = total
            return 0

        lax.fori_loop(0, 32, long_filter, 0)

        def first_factor(g, _):
            rows = []
            for part in range(2):
                even, odd = [], []
                for q2 in range(2):
                    a = fl[pl.ds(g * 256 + part * 4 + 2 * q2, 32, stride=8), :]
                    b = fl[pl.ds(g * 256 + part * 4 + 2 * q2 + 1, 32, stride=8), :]
                    even.append(jnp.where(low, a, pltpu.roll(b, RADIX, 1)))
                    odd.append(jnp.where(low, pltpu.roll(a, RADIX, 1), b))
                rows.append(jnp.concatenate(even, axis=1))
                rows.append(jnp.concatenate(odd, axis=1))
            out = dot(first[...], jnp.concatenate(rows, axis=0).astype(BF))
            real, imag = out[:RADIX], out[RADIX:]
            at = pl.ds(pl.multiple_of(g * RADIX, RADIX), RADIX)
            tw[at, 0:256] = (real * twist[0] + imag * twist[1]).astype(BF)
            tw[at, 256:512] = (imag * twist[0] - real * twist[1]).astype(BF)
            return 0

        lax.fori_loop(first_frame, first_frame + frames, first_factor, 0)

        def second_factor(rows):
            return dot_t(second[...], rows).reshape(STN, 8, LANES)

        if c == 0:
            send_half[...] = second_factor(tw[8 * RADIX : 10 * RADIX, :]).astype(BF)
            send_all(*half_args)
            tail_tw[96:128, :] = tw[640:672, :]
            tail_tw[224:256, :] = tw[672:704, :]
            tail = [second_factor(tail_tw[e * LANES : (e + 1) * LANES, :]) for e in range(2)]
            short_spectra(2, jnp.concatenate(tail, axis=1))
            send_all(*beam_args[2])
        else:
            pairs = [
                second_factor(tw[at : at + LANES, :])
                for at in (first_frame * RADIX, first_frame * RADIX + LANES)
            ]
            send_spec[c - 1] = jnp.concatenate(pairs, axis=1).astype(BF)
            if c == 1:
                send_all(*spec_args[0])
            else:
                send_all(*spec_args[1], 1, LATE)
                send_all(send_spec.at[1], recv_spec.at[1], late_sem, spec_recv_sem.at[1], LATE, STN)

    shape = (256, 1024)
    column = lax.broadcasted_iota(jnp.int32, shape, 1)
    match = lax.broadcasted_iota(jnp.int32, shape, 0) == stn * 4 + (column // 2) % 4
    own_re = jnp.where(match & (column % 2 == 0), 1.0, 0.0).astype(BF)
    own_im = jnp.where(match & (column % 2 == 1), 1.0, 0.0).astype(BF)
    factor = 1.0 / math.sqrt(2 * STN)
    cos = (jnp.cos(angles[...]) * factor).astype(BF)
    sin = (jnp.sin(angles[...]) * factor).astype(BF)
    table[0] = dot(cos, own_re) - dot(sin, own_im)
    table[1] = dot(sin, own_re) + dot(cos, own_im)
    shape = (128, 1024)
    spread = jnp.where(
        lax.broadcasted_iota(jnp.int32, shape, 0) == lax.broadcasted_iota(jnp.int32, shape, 1) // 8,
        1.0,
        0.0,
    ).astype(BF)
    chosen = dot(index[...].astype(F32).astype(BF), spread)

    def choose(t, carry):
        real, imag = carry
        hit = chosen == t.astype(F32)
        return (
            jnp.where(hit, jnp.broadcast_to(table[0, pl.ds(t, 1), :], (16, 1024)), real),
            jnp.where(hit, jnp.broadcast_to(table[1, pl.ds(t, 1), :], (16, 1024)), imag),
        )

    zero = jnp.zeros((16, 1024), F32)
    chosen_parts = lax.fori_loop(0, 64, choose, (zero, zero))
    channel = (lax.broadcasted_iota(jnp.int32, (16, 1024), 1) // 2) % 4
    for po in range(2):
        for ci in range(4):
            weights[po * 64 + ci * 16 : po * 64 + ci * 16 + 16, :] = jnp.where(
                channel == ci, chosen_parts[po], 0.0
            ).astype(BF)

    def beam_power(c):
        first_frame, frames = BEAM_GROUPS[c]
        wait_all(*beam_args[c])
        fields = dot(weights[...], recv_beam[c].reshape(1024, LANES))
        power = fields[:64] * fields[:64] + fields[64:] * fields[64:]
        power_ref[:, first_frame : first_frame + frames] = power[:, :frames] + power[:, frames : 2 * frames]

    def hand_over(k):
        other = lax.rem(grp + k, GRP)
        return pltpu.make_async_remote_copy(
            src_ref=part_send.at[other],
            dst_ref=part_recv.at[k - 1],
            send_sem=part_send_sem.at[k - 1],
            recv_sem=part_recv_sem.at[k - 1],
            device_id=(stn, other),
            device_id_type=MESH,
        )

    def correlate(source, selection, pairs, masked, first_block, last_block):
        rows_each = source.shape[1]

        def gather_rows(b, _):
            block = source[pl.ds(b * 16, 16)].reshape(16 * rows_each, LANES)
            rows = dot(selection[...], block)
            if masked:
                rows = jnp.where(lax.broadcasted_iota(jnp.int32, rows.shape, 1) >= 96, rows, 0.0)
            rows = rows.astype(BF)
            wide = pl.ds(pl.multiple_of(b * 128, 128), 128)
            narrow = pl.ds(pl.multiple_of(b * 64, 64), 64)
            for e in range(pairs):
                at = 384 * e
                lanes = 2 * e * LANES
                lhs[wide, lanes : lanes + LANES] = rows[at : at + 128]
                lhs[wide, lanes + LANES : lanes + 2 * LANES] = rows[at + 128 : at + 256]
                rhs[narrow, lanes : lanes + LANES] = rows[at + 256 : at + 320]
                rhs[narrow, lanes + LANES : lanes + 2 * LANES] = rows[at + 320 : at + 384]
            return 0

        lax.fori_loop(0, 4, gather_rows, 0)
        depth = 2 * pairs * LANES
        for k in (1, 2, 3, 0):
            owner = lax.rem(grp + k, GRP)
            partial = dot_t(lhs[pl.ds(pl.multiple_of(owner * 128, 128), 128), 0:depth], rhs[:, 0:depth])
            if not first_block:
                partial = partial + part_own[k]
            if not last_block or k == 0:
                part_own[k] = partial
            else:
                part_send[owner] = partial.astype(BF)
                hand_over(k).start()

    wait_all(*half_args)
    correlate(recv_half, pick_half, 1, False, True, False)
    beam_power(2)
    correlate(recv_beam.at[2], pick, 2, True, False, False)
    wait_all(*spec_args[0])
    correlate(recv_spec.at[0], pick, 2, False, False, False)
    pltpu.make_async_copy(
        send_spec.at[1, pl.ds(0, LATE - 1)], recv_spec.at[1, pl.ds(0, LATE - 1)], spec_send_sem.at[1]
    ).wait()
    send_all(*beam_args[1], STN // 2, STN)
    send_all(*beam_args[0], 48, STN)
    wait_all(*spec_args[1])
    correlate(recv_spec.at[1], pick, 2, False, False, True)

    beam_power(1)
    beam_power(0)

    total = part_own[0]
    for k in range(1, GRP):
        hand_over(k).wait_recv()
        total = total + part_recv[k - 1].astype(F32)
    total = total * (1.0 / math.sqrt(4 * FRAMES * RADIX))
    for u in range(64):
        vis_ref[0, u] = total[2 * u : 2 * u + 2]

    for k in range(1, GRP):
        hand_over(k).wait_send()
    for c in range(3):
        wait_sent(*beam_args[c])
    wait_sent(*half_args)
    wait_sent(*spec_args[0])
    pltpu.make_async_copy(
        send_spec.at[1, pl.ds(0, STN - LATE)], recv_spec.at[1, pl.ds(0, STN - LATE)], late_sem
    ).wait()

    @pl.when(grp < GRP - 1)
    def _():
        for c in range(3):
            halo(c).wait_send()


def on_device(voltages, corr_taps, beam_taps, angle_table, table_index):
    volts = voltages.reshape(4, 2, TILES * LANES)
    tables = [jnp.asarray(t) for t in constant_tables()]
    vmem = pl.BlockSpec(memory_space=pltpu.VMEM)
    dma = pltpu.SemaphoreType.DMA
    vis, power = pl.pallas_call(
        kernel,
        out_shape=(
            jax.ShapeDtypeStruct((1, 64, 2, 256), F32),
            jax.ShapeDtypeStruct((64, SHORT_FRAMES), F32),
        ),
        in_specs=[pl.BlockSpec(memory_space=pl.ANY)] * 11,
        out_specs=(vmem, vmem),
        scratch_shapes=[
            pltpu.VMEM((512, 512), BF),
            pltpu.VMEM((512, 512), BF),
            pltpu.VMEM((768, 256), BF),
            pltpu.VMEM((384, LANES), BF),
            pltpu.VMEM((4, 2, TILES * LANES), BF),
            pltpu.VMEM((TAPS, RADIX * RADIX), F32),
            pltpu.VMEM((TAPS, 256), F32),
            pltpu.VMEM((64, 256), F32),
            pltpu.VMEM((16, 128), jnp.int32),
            pltpu.VMEM((128, 128), BF),
            pltpu.VMEM((2, 64, 256), F32),
            pltpu.VMEM((HALF, 16, LANES), BF),
            pltpu.VMEM((HALF, 16, LANES), BF),
            pltpu.VMEM((2 * TILES, 8, LANES), F32),
            pltpu.VMEM((2, SHORT_FRAMES * 8, LANES), F32),
            pltpu.VMEM((FRAMES * 256, LANES), F32),
            pltpu.VMEM((LANES, 512), BF),
            pltpu.VMEM((FRAMES * RADIX, 512), BF),
            pltpu.VMEM((2 * LANES, 512), BF),
            pltpu.VMEM((3, STN, 16, LANES), BF),
            pltpu.VMEM((3, STN, 16, LANES), BF),
            pltpu.VMEM((2, STN, 16, LANES), BF),
            pltpu.VMEM((2, STN, 16, LANES), BF),
            pltpu.VMEM((STN, 8, LANES), BF),
            pltpu.VMEM((STN, 8, LANES), BF),
            pltpu.VMEM((2, 64, 1024), F32),
            pltpu.VMEM((128, 1024), BF),
            pltpu.VMEM((512, 512), BF),
            pltpu.VMEM((256, 512), BF),
            pltpu.VMEM((GRP, 128, 256), F32),
            pltpu.VMEM((GRP, 128, 256), BF),
            pltpu.VMEM((GRP - 1, 128, 256), BF),
            pltpu.SemaphoreType.REGULAR,
            pltpu.SemaphoreType.REGULAR,
            dma((11,)),
            dma((3,)),
            dma((3,)),
            dma((3,)),
            dma((3,)),
            dma((2,)),
            dma((2,)),
            dma,
            dma,
            dma,
            dma((GRP - 1,)),
            dma((GRP - 1,)),
        ],
        compiler_params=pltpu.CompilerParams(
            collective_id=0, has_side_effects=True, vmem_limit_bytes=60 * 1024 * 1024
        ),
    )(volts, corr_taps, beam_taps, angle_table, table_index, *tables)
    return vis, power.reshape(4, 16, SHORT_FRAMES)


def solution(mesh):
    in_specs = (P(None, "stn", None, "grp"), P(), P(), P(), P())
    out_specs = (P("stn", "grp", None, None), P("stn", None, "grp"))
    return jax.shard_map(
        on_device, mesh=mesh, in_specs=in_specs, out_specs=out_specs, check_vma=False
    )
```
